1024 devices in a mesh: lat: 32 (over y_hi, z), lon: 32 (over x, y_lo, core).
Axes of the slice: x: 4, y: 8 (y_hi: 2, y_lo: 4; y = y_hi * 4 + y_lo), z: 16, core: 2. Of those that a mesh axis runs over, the one named last changes fastest.
Arguments:
- vector: bfloat16 [8, 72, 32, 4096], P(None, None, 'lat', 'lon'), may hold values from -6 to 6
- obs_weight: float32 [72, 32, 4096], P(None, 'lat', 'lon'), may hold values from 0.2 to 5
- departures: int32 [4, 32, 32], P(None, 'lat', 'lon'), may hold values from 0 to 2
- weight_index: int32 [4, 32, 32], P(None, 'lat', 'lon'), may hold values from 0 to 15
- interp_table: bfloat16 [16, 160, 128], replicated, may hold values from -0.5 to 0.5
- column_mix: bfloat16 [4, 32, 72, 72], P(None, 'lat'), may hold values from -0.75 to 0.75
Outputs:
- hess_vec: bfloat16 [8, 72, 32, 4096], P(None, None, 'lat', 'lon')
The draws below stay inside these ranges and needn't reach their ends.
Inputs may be any that keep to these rules, and one draw needn't show every extreme that they name: `departures`: 0 names the row above the reader row, 1 the reader row, 2 the row below. `weight_index`: an entry of the first dimension of interp_table.
All inputs are finite; a program needn't handle non-finite values.
Results may differ from the reference program's by a relative error of at most 0.022.
Values may be sent and summed in bfloat16 or wider, within the bound.
No kernel may reach another device: no remote copies, remote signals or barrier semaphores. Data moves between devices by JAX's collectives and lax.ppermute only.
A program may use at most 32 MiB of HBM per device.

```python
import math
import jax
import jax.numpy as jnp
from jax import lax

TRAC = 8
LEV = 72
CLON = 128
REACH = 16
NWT = 16
STEPS = 4
NLAT = 32
NLON = 4096
LONB = 32


def touch_ends(entries, key, least, largest):
    shape = entries.shape
    place = [jax.random.randint(jax.random.fold_in(key, axis), (), 0, shape[axis]) for axis in range(len(shape))]
    entries = entries.at[tuple(place)].set(least)
    longest = shape.index(max(shape))
    place[longest] = (place[longest] + 1) % shape[longest]
    return entries.at[tuple(place)].set(largest)


def shard_levels(rng, shape, shards, smallest, top_value):
    def one(position, shards_of):
        heights = jax.random.uniform(jax.random.fold_in(jax.random.fold_in(rng, 6), position), (shards_of,), jnp.float32, smallest / len(shards), top_value / len(shards))
        return jnp.repeat(jnp.exp(heights), shape[position] // shards_of).reshape((-1,) + (1,) * (len(shape) - position - 1))

    gain = one(*shards[0])
    for cut in shards[1:]:
        gain = gain * one(*cut)
    return gain


def bell_draw(key, dims, width, limit, pieces=(), kind=jnp.bfloat16):
    entries = jax.random.normal(key, dims, jnp.float32) * width
    if len(pieces) > 0:
        entries = shard_levels(key, dims, pieces, -0.22, 0.18) * entries
    return jnp.clip(entries, min=-limit, max=limit).astype(kind)


def setup_inputs(seed: int = 0) -> dict:
    key_of = jax.random.split(jax.random.key(seed), 7)
    vector = bell_draw(key_of[0], (TRAC, LEV, NLAT, NLON), 1.0, 6.0, ((2, 32), (3, 32)))
    obs_weight = jnp.clip(jnp.exp(math.log(5.0) - 3.218876 * jax.random.uniform(key_of[1], (LEV, NLAT, NLON), jnp.float32) ** shard_levels(key_of[1], (LEV, NLAT, NLON), ((1, 32), (2, 32)), -0.2, 0.2)), 0.2, 5.0)
    departures = touch_ends(jax.random.randint(key_of[2], (STEPS, NLAT, LONB), 0, 3), jax.random.fold_in(key_of[2], 1), 0, 2).astype(jnp.int32)
    weight_index = touch_ends(jax.random.randint(key_of[3], (STEPS, NLAT, LONB), 0, NWT), jax.random.fold_in(key_of[3], 1), 0, NWT - 1).astype(jnp.int32)
    interp_table = bell_draw(key_of[4], (NWT, CLON + 2 * REACH, CLON), (CLON + 2 * REACH) ** -0.5, 0.5)
    column_mix = bell_draw(key_of[5], (STEPS, NLAT, LEV, LEV), LEV ** -0.5, 0.75, ((1, 32),))
    return {"vector": vector, "obs_weight": obs_weight, "departures": departures, "weight_index": weight_index, "interp_table": interp_table, "column_mix": column_mix}


def tangent_step(tracer_field, offsets, weight_rows, interp_table, mixing):
    block_cols = interp_table.shape[2]
    lon_reach = (interp_table.shape[1] - block_cols) // 2
    blocks = offsets.shape[1]
    wrapped = jnp.concatenate([tracer_field[..., -lon_reach:], tracer_field, tracer_field[..., :lon_reach]], axis=3)
    padded = jnp.pad(wrapped, ((0, 0), (0, 0), (1, 1), (0, 0)))
    row_ids = jnp.arange(tracer_field.shape[2], dtype=jnp.int32)
    mixing_f = mixing.astype(jnp.float32)

    def one_block(block_id):
        window = lax.dynamic_slice_in_dim(padded, block_id * block_cols, block_cols + 2 * lon_reach, axis=3)
        source_rows = (row_ids + offsets[:, block_id]).astype(jnp.int32)
        picked = jnp.take(window, source_rows, axis=2)
        weights = jnp.take(interp_table, weight_rows[:, block_id], axis=0)
        interp = jnp.einsum('tlrj,rjc->tlrc', picked.astype(jnp.float32), weights.astype(jnp.float32)).astype(jnp.bfloat16)
        mixed_cols = jnp.einsum('rkl,tlrc->tkrc', mixing_f, interp.astype(jnp.float32))
        return mixed_cols.astype(jnp.bfloat16)

    stacked = lax.map(one_block, jnp.arange(blocks, dtype=jnp.int32))
    stacked = jnp.moveaxis(stacked, 0, 3)
    return stacked.reshape(tracer_field.shape)


def adjoint_step(cotangent, offsets, weight_rows, interp_table, mixing):
    block_cols = interp_table.shape[2]
    lon_reach = (interp_table.shape[1] - block_cols) // 2
    blocks = offsets.shape[1]
    tracers, levels, nrows, ncols = cotangent.shape
    row_ids = jnp.arange(nrows, dtype=jnp.int32)
    mixing_f = mixing.astype(jnp.float32)
    accumulated = jnp.zeros((tracers, levels, nrows + 2, ncols + 2 * lon_reach), jnp.float32)

    def add_block(block_id, accumulated):
        cot_slab = lax.dynamic_slice_in_dim(cotangent, block_id * block_cols, block_cols, axis=3)
        back_mixed = jnp.einsum('rkl,tkrc->tlrc', mixing_f, cot_slab.astype(jnp.float32)).astype(jnp.bfloat16)
        weights = jnp.take(interp_table, weight_rows[:, block_id], axis=0)
        spread = jnp.einsum('tlrc,rjc->tlrj', back_mixed.astype(jnp.float32), weights.astype(jnp.float32))
        source_rows = (row_ids + offsets[:, block_id]).astype(jnp.int32)
        lifted = jnp.zeros((tracers, levels, nrows + 2, block_cols + 2 * lon_reach), jnp.float32)
        lifted = lifted.at[:, :, source_rows, :].add(spread)
        current = lax.dynamic_slice_in_dim(accumulated, block_id * block_cols, block_cols + 2 * lon_reach, axis=3)
        return lax.dynamic_update_slice_in_dim(accumulated, current + lifted, block_id * block_cols, axis=3)

    accumulated = lax.fori_loop(0, blocks, add_block, accumulated)
    interior = accumulated[:, :, 1:-1, :]
    folded = interior[..., lon_reach:lon_reach + ncols]
    folded = folded.at[..., :lon_reach].add(interior[..., lon_reach + ncols:])
    folded = folded.at[..., ncols - lon_reach:].add(interior[..., :lon_reach])
    return folded.astype(jnp.bfloat16)


def reference(vector, obs_weight, departures, weight_index, interp_table, column_mix):
    tracer_state = vector
    for moment in range(STEPS):
        tracer_state = tangent_step(tracer_state, departures[moment], weight_index[moment], interp_table, column_mix[moment])
    adjoint = (obs_weight[None] * tracer_state.astype(jnp.float32)).astype(jnp.bfloat16)
    for moment in reversed(range(STEPS)):
        adjoint = adjoint_step(adjoint, departures[moment], weight_index[moment], interp_table, column_mix[moment])
    return adjoint
```

```python
import functools

import jax
import jax.numpy as jnp
from jax import lax
from jax.experimental import pallas as pl
from jax.experimental.pallas import tpu as pltpu
from jax.sharding import PartitionSpec as P

F32, BF16 = jnp.float32, jnp.bfloat16
VMEM = pl.BlockSpec(memory_space=pltpu.VMEM)
SMEM = pl.BlockSpec(memory_space=pltpu.SMEM)
LIMIT = 24 * 1024 * 1024


def right_lanes(shape):
    return lax.broadcasted_iota(jnp.int32, shape, 1) < shape[1] // 2


def forward_kernel(step, first, outs, fold, weighted, par, own, north, south, table, mix, *rest):
    obs, out = rest if weighted else (None, rest[0])
    shape = own.shape[1:]
    rightward = right_lanes(shape)
    blocks = []
    for p in range(outs):
        way, which = par[step, first + p], par[4 + step, first + p]

        def pick(j):
            return jnp.where(way == 1, own[j], jnp.where(way == 0, north[j], south[j]))

        left = p - 1 if p > 0 else outs
        right = p + 1 if p < outs - 1 else outs
        edges = jnp.where(rightward, pick(right), pick(left))
        window = jnp.concatenate([pick(p), edges], axis=1)
        interp = jnp.dot(window, table[which], preferred_element_type=F32).astype(BF16)
        mixed = jnp.dot(mix[step, 0], interp, preferred_element_type=F32).astype(BF16)
        if weighted:
            mixed = (obs[p].astype(F32) * mixed.astype(F32)).astype(BF16)
        if fold and p in (0, outs - 1):
            blocks.append(mixed)
        else:
            out[p - 1 if fold else p] = mixed
    if fold:
        out[outs - 2] = jnp.where(rightward, blocks[1], blocks[0])


def forward(step, outs, fold, par, rows, table, mix, obs=None):
    levels, cols = rows[0].shape[1:]
    first = (par.shape[1] - outs) // 2
    made = outs - 1 if fold else outs
    weighted = obs is not None
    args = (par, *rows, table, mix) + ((obs,) if weighted else ())
    return pl.pallas_call(
        functools.partial(forward_kernel, step, first, outs, fold, weighted),
        out_shape=jax.ShapeDtypeStruct((made, levels, cols), BF16),
        in_specs=[SMEM] + [VMEM] * (len(args) - 1),
        out_specs=VMEM,
        compiler_params=pltpu.CompilerParams(vmem_limit_bytes=LIMIT),
        cost_estimate=pl.CostEstimate(flops=outs * 6_000_000, bytes_accessed=2_000_000, transcendentals=0),
    )(*args)


def adjoint_kernel(step, first, reads, summed, par, *rest):
    parts, (table, mix, to_north, stay, to_south, total) = rest[: 3 if summed else 1], rest[3 if summed else 1 :]
    shape = parts[0].shape[1:]
    rightward = right_lanes(shape)
    nothing = jnp.zeros(shape, F32)
    for way in range(3):
        for p in range(reads):
            total[way, p] = nothing
    for p in range(reads):
        way, which = par[step, first + p], par[4 + step, first + p]
        if summed:
            cot = (parts[0][p] + parts[1][p].astype(F32) + parts[2][p].astype(F32)).astype(BF16)
        else:
            cot = parts[0][p]
        back = lax.dot_general(mix[step, 0], cot, (((0,), (0,)), ((), ())), preferred_element_type=F32).astype(BF16)
        spread = jnp.dot(back, table[which], preferred_element_type=F32)
        main, edges = spread[:, : shape[1]], spread[:, shape[1] :]
        if 0 < p < reads - 1:
            total[way, p] += main
        if p < reads - 2:
            total[way, p + 1] += jnp.where(rightward, edges, nothing)
        if p > 1:
            total[way, p - 1] += jnp.where(rightward, nothing, edges)
    for p in range(1, reads - 1):
        to_north[p - 1] = total[0, p].astype(BF16)
        stay[p - 1] = total[1, p]
        to_south[p - 1] = total[2, p].astype(BF16)


def adjoint(step, par, parts, table, mix):
    reads, levels, cols = parts[0].shape
    first = (par.shape[1] - reads) // 2
    gives = (reads - 2, levels, cols)
    return pl.pallas_call(
        functools.partial(adjoint_kernel, step, first, reads, len(parts) == 3),
        out_shape=[jax.ShapeDtypeStruct(gives, BF16), jax.ShapeDtypeStruct(gives, F32), jax.ShapeDtypeStruct(gives, BF16)],
        in_specs=[SMEM] + [VMEM] * (len(parts) + 2),
        out_specs=[VMEM] * 3,
        scratch_shapes=[pltpu.VMEM((3, reads, levels, cols), F32)],
        compiler_params=pltpu.CompilerParams(vmem_limit_bytes=LIMIT),
        cost_estimate=pl.CostEstimate(flops=reads * 6_000_000, bytes_accessed=2_000_000, transcendentals=0),
    )(par, *parts, table, mix)


def from_lat(value, by):
    length = lax.axis_size("lat")
    return lax.ppermute(value, "lat", [(i, i - by) for i in range(length) if 0 <= i - by < length])


def from_lon(value, by):
    length = lax.axis_size("lon")
    return lax.ppermute(value, "lon", [(i, (i - by) % length) for i in range(length)])


def exchange(value, run):
    length = lax.axis_size("lon")
    groups = [list(range(i, i + run)) for i in range(0, length, run)]
    return lax.all_to_all(value, "lon", 0, 0, axis_index_groups=groups)


def on_device(vector, obs_weight, departures, weight_index, interp_table, column_mix):
    run, levels, _, cols = vector.shape
    reach = (interp_table.shape[1] - cols) // 2
    inner = interp_table[:, reach : reach + cols]
    gap = jnp.zeros((interp_table.shape[0], cols - 2 * reach, cols), BF16)
    table = jnp.concatenate([inner, interp_table[:, reach + cols :], gap, interp_table[:, :reach]], axis=1)
    table_t = jnp.swapaxes(table, 1, 2)

    numbers = jnp.concatenate([departures.reshape(-1), weight_index.reshape(-1)]).astype(BF16)
    count = numbers.shape[0]
    tail = jnp.concatenate([jnp.broadcast_to(numbers[:, None], (count, cols)), jnp.zeros((16 - count, cols), BF16)])
    shared = jnp.concatenate([obs_weight[:, 0].astype(BF16), tail])
    bundle = jnp.concatenate(
        [vector[:, :, 0], jnp.broadcast_to(shared[None], (run, *shared.shape))], axis=1
    )
    bundle = exchange(bundle, run)
    state, obs = bundle[:, :levels], bundle[:, levels : 2 * levels]
    ends = jnp.concatenate([state, bundle[:, 2 * levels :]], axis=1)
    west, east = from_lon(ends[-2:], -run), from_lon(ends[:2], run)
    values = jnp.concatenate(
        [west[:, levels : levels + count, 0], bundle[:, 2 * levels : 2 * levels + count, 0], east[:, levels : levels + count, 0]]
    )
    par = values.astype(jnp.int32).T
    west, east = west[:, :levels], east[:, :levels]

    for step in range(0, 4, 2):
        if step > 0:
            west, east = from_lon(state[-2:], -run), from_lon(state[:2], run)
        rightward = right_lanes((levels, cols))
        outer = jnp.where(rightward, east[1], west[0])
        wide = jnp.concatenate([west[1:], state, east[:1], outer[None]])
        wide = forward(step, run + 2, True, par, (wide, from_lat(wide, -1), from_lat(wide, 1)), table, column_mix)
        state = forward(
            step + 1, run, False, par, (wide, from_lat(wide, -1), from_lat(wide, 1)), table, column_mix,
            obs if step == 2 else None,
        )

    cot = state
    for step in (3, 1):
        west, east = from_lon(cot[-2:], -run), from_lon(cot[:2], run)
        wide = jnp.concatenate([west, cot, east])
        north, stay, south = adjoint(step, par, (wide,), table_t, column_mix)
        parts = (stay, from_lat(north, 1), from_lat(south, -1))
        north, stay, south = adjoint(step - 1, par, parts, table_t, column_mix)
        cot = (stay + from_lat(north, 1).astype(F32) + from_lat(south, -1).astype(F32)).astype(BF16)
    return exchange(cot, run)[:, :, None]


def solution(mesh):
    placed = (
        P(None, None, "lat", "lon"),
        P(None, "lat", "lon"),
        P(None, "lat", "lon"),
        P(None, "lat", "lon"),
        P(),
        P(None, "lat", None, None),
    )
    return jax.shard_map(
        on_device, mesh=mesh, in_specs=placed, out_specs=P(None, None, "lat", "lon"), check_vma=False
    )
```

```python
import functools

import jax
import jax.numpy as jnp
from jax import lax
from jax.experimental import pallas as pl
from jax.experimental.pallas import tpu as pltpu
from jax.sharding import PartitionSpec as P

F32, BF16 = jnp.float32, jnp.bfloat16
VMEM = pl.BlockSpec(memory_space=pltpu.VMEM)
SMEM = pl.BlockSpec(memory_space=pltpu.SMEM)
LIMIT = 24 * 1024 * 1024


def right_lanes(shape):
    return lax.broadcasted_iota(jnp.int32, shape, 1) < shape[1] // 2


def window_weights(table, which):
    weights = table[which]
    cols = weights.shape[1]
    reach = (weights.shape[0] - cols) // 2
    gap = jnp.zeros((cols - 2 * reach, cols), weights.dtype)
    return jnp.concatenate([weights[reach : reach + cols], weights[reach + cols :], gap, weights[:reach]], axis=0)


def forward_kernel(step, first, outs, fold, weighted, par, own, north, south, table, mix, *rest):
    obs, out = rest if weighted else (None, rest[0])
    shape = own.shape[1:]
    rightward = right_lanes(shape)
    blocks = []
    for p in range(outs):
        way, which = par[first + p, step], par[first + p, 4 + step]

        def pick(j):
            return jnp.where(way == 1, own[j], jnp.where(way == 0, north[j], south[j]))

        left = p - 1 if p > 0 else outs
        right = p + 1 if p < outs - 1 else outs
        edges = jnp.where(rightward, pick(right), pick(left))
        window = jnp.concatenate([pick(p), edges], axis=1)
        interp = jnp.dot(window, window_weights(table, which), preferred_element_type=F32).astype(BF16)
        mixed = jnp.dot(mix[step][:, : shape[0]], interp, preferred_element_type=F32).astype(BF16)
        if weighted:
            mixed = (obs[p].astype(F32) * mixed.astype(F32)).astype(BF16)
        if fold and p in (0, outs - 1):
            blocks.append(mixed)
        else:
            out[p - 1 if fold else p] = mixed
    if fold:
        out[outs - 2] = jnp.where(rightward, blocks[1], blocks[0])


def forward(step, outs, fold, par, rows, table, mix, obs=None):
    levels, cols = rows[0].shape[1:]
    first = (par.shape[0] - outs) // 2
    made = outs - 1 if fold else outs
    weighted = obs is not None
    args = (par, *rows, table, mix) + ((obs,) if weighted else ())
    return pl.pallas_call(
        functools.partial(forward_kernel, step, first, outs, fold, weighted),
        out_shape=jax.ShapeDtypeStruct((made, levels, cols), BF16),
        in_specs=[SMEM] + [VMEM] * (len(args) - 1),
        out_specs=VMEM,
        compiler_params=pltpu.CompilerParams(vmem_limit_bytes=LIMIT),
        cost_estimate=pl.CostEstimate(flops=outs * 6_000_000, bytes_accessed=2_000_000, transcendentals=0),
    )(*args)


def adjoint_kernel(step, first, reads, summed, par, *rest):
    parts, (table, mix, to_north, stay, to_south, total) = rest[: 3 if summed else 1], rest[3 if summed else 1 :]
    shape = parts[0].shape[1:]
    rightward = right_lanes(shape)
    nothing = jnp.zeros(shape, F32)
    for way in range(3):
        for p in range(reads):
            total[way, p] = nothing
    for p in range(reads):
        way, which = par[first + p, step], par[first + p, 4 + step]
        if summed:
            cot = (parts[0][p] + parts[1][p].astype(F32) + parts[2][p].astype(F32)).astype(BF16)
        else:
            cot = parts[0][p]
        back = lax.dot_general(mix[step][:, : shape[0]], cot, (((0,), (0,)), ((), ())), preferred_element_type=F32).astype(BF16)
        spread = lax.dot_general(back, window_weights(table, which), (((1,), (1,)), ((), ())), preferred_element_type=F32)
        main, edges = spread[:, : shape[1]], spread[:, shape[1] :]
        if 0 < p < reads - 1:
            total[way, p] += main
        if p < reads - 2:
            total[way, p + 1] += jnp.where(rightward, edges, nothing)
        if p > 1:
            total[way, p - 1] += jnp.where(rightward, nothing, edges)
    for p in range(1, reads - 1):
        to_north[p - 1] = total[0, p].astype(BF16)
        stay[p - 1] = total[1, p]
        to_south[p - 1] = total[2, p].astype(BF16)


def adjoint(step, par, parts, table, mix):
    reads, levels, cols = parts[0].shape
    first = (par.shape[0] - reads) // 2
    gives = (reads - 2, levels, cols)
    return pl.pallas_call(
        functools.partial(adjoint_kernel, step, first, reads, len(parts) == 3),
        out_shape=[jax.ShapeDtypeStruct(gives, BF16), jax.ShapeDtypeStruct(gives, F32), jax.ShapeDtypeStruct(gives, BF16)],
        in_specs=[SMEM] + [VMEM] * (len(parts) + 2),
        out_specs=[VMEM] * 3,
        scratch_shapes=[pltpu.VMEM((3, reads, levels, cols), F32)],
        compiler_params=pltpu.CompilerParams(vmem_limit_bytes=LIMIT),
        cost_estimate=pl.CostEstimate(flops=reads * 6_000_000, bytes_accessed=2_000_000, transcendentals=0),
    )(par, *parts, table, mix)


def homes():
    half, run = lax.axis_size("lat") // 2, 8
    rows, blocks = lax.axis_size("lat"), lax.axis_size("lon")

    def home(row, block):
        upper, z = divmod(row, half)
        column, slot = divmod(block, run)
        y, core = divmod(slot, 2)
        return (core * half + z - z % 2 + upper) * blocks + column * run + y * 2 + z % 2

    return rows, blocks, home


def move(value, pairs):
    return lax.ppermute(value, ("lat", "lon"), pairs)


def go_home(value, back=False):
    rows, blocks, home = homes()
    pairs = [(r * blocks + b, home(r, b)) for r in range(rows) for b in range(blocks)]
    return move(value, [(t, s) for s, t in pairs] if back else pairs)


def from_lat(value, by):
    rows, blocks, home = homes()
    return move(value, [(home(r, b), home(r - by, b)) for r in range(rows) for b in range(blocks) if 0 <= r - by < rows])


def from_lon(value, by):
    rows, blocks, home = homes()
    return move(value, [(home(r, b), home(r, (b - by) % blocks)) for r in range(rows) for b in range(blocks)])


def exchange(value, run):
    rows, blocks, home = homes()
    groups = [[home(r, b + j) for j in range(run)] for r in range(rows) for b in range(0, blocks, run)]
    return lax.all_to_all(value, ("lat", "lon"), 0, 0, axis_index_groups=groups)


def on_device(vector, obs_weight, departures, weight_index, interp_table, column_mix):
    run, levels, _, cols = vector.shape
    numbers = jnp.concatenate([departures.reshape(-1), weight_index.reshape(-1)]).astype(BF16)
    count = numbers.shape[0]
    tail = jnp.concatenate([jnp.broadcast_to(numbers[:, None], (count, cols)), jnp.zeros((16 - count, cols), BF16)])
    mix = jnp.pad(column_mix[:, 0], ((0, 0), (0, 0), (0, cols - levels)))
    steps = mix.shape[0]
    sent = jnp.concatenate([vector.reshape(-1, cols), mix.reshape(-1, cols), obs_weight[:, 0].astype(BF16), tail])
    sent = go_home(sent)
    mix = sent[run * levels : (run + steps) * levels].reshape(steps, levels, cols)
    shared = sent[(run + steps) * levels :]
    bundle = jnp.concatenate(
        [sent[: run * levels].reshape(run, levels, cols), jnp.broadcast_to(shared[None], (run, *shared.shape))], axis=1
    )
    bundle = exchange(bundle, run)
    state, obs = bundle[:, :levels], bundle[:, levels : 2 * levels]
    west, east = from_lon(bundle[-2:], -run), from_lon(bundle[:2], run)

    def read(part):
        return jnp.max(part[:, 2 * levels : 2 * levels + count].astype(F32), axis=2).astype(jnp.int32)

    par = jnp.concatenate([read(west), read(bundle), read(east)])
    west, east = west[:, :levels], east[:, :levels]

    for step in range(0, 4, 2):
        if step > 0:
            west, east = from_lon(state[-2:], -run), from_lon(state[:2], run)
        rightward = right_lanes((levels, cols))
        outer = jnp.where(rightward, east[1], west[0])
        wide = jnp.concatenate([west[1:], state, east[:1], outer[None]])
        wide = forward(step, run + 2, True, par, (wide, from_lat(wide, -1), from_lat(wide, 1)), interp_table, mix)
        state = forward(
            step + 1, run, False, par, (wide, from_lat(wide, -1), from_lat(wide, 1)), interp_table, mix,
            obs if step == 2 else None,
        )

    cot = state
    for step in (3, 1):
        west, east = from_lon(cot[-2:], -run), from_lon(cot[:2], run)
        wide = jnp.concatenate([west, cot, east])
        north, stay, south = adjoint(step, par, (wide,), interp_table, mix)
        parts = (stay, from_lat(north, 1), from_lat(south, -1))
        north, stay, south = adjoint(step - 1, par, parts, interp_table, mix)
        cot = (stay + from_lat(north, 1).astype(F32) + from_lat(south, -1).astype(F32)).astype(BF16)
    return go_home(exchange(cot, run), back=True)[:, :, None]


def solution(mesh):
    placed = (
        P(None, None, "lat", "lon"),
        P(None, "lat", "lon"),
        P(None, "lat", "lon"),
        P(None, "lat", "lon"),
        P(),
        P(None, "lat", None, None),
    )
    return jax.shard_map(
        on_device, mesh=mesh, in_specs=placed, out_specs=P(None, None, "lat", "lon"), check_vma=False
    )
```

```python
import functools

import jax
import jax.numpy as jnp
from jax import lax
from jax.experimental import pallas as pl
from jax.experimental.pallas import tpu as pltpu
from jax.sharding import PartitionSpec as P

F32, BF16 = jnp.float32, jnp.bfloat16
VMEM = pl.BlockSpec(memory_space=pltpu.VMEM)
SMEM = pl.BlockSpec(memory_space=pltpu.SMEM)
LIMIT = 24 * 1024 * 1024


def right_lanes(shape):
    return lax.broadcasted_iota(jnp.int32, shape, 1) < shape[1] // 2


def window_weights(table, which):
    weights = table[which]
    cols = weights.shape[1]
    reach = (weights.shape[0] - cols) // 2
    gap = jnp.zeros((cols - 2 * reach, cols), weights.dtype)
    return jnp.concatenate([weights[reach : reach + cols], weights[reach + cols :], gap, weights[:reach]], axis=0)


def forward_kernel(step, first, outs, fold, weighted, par, own, north, south, table, mix, *rest):
    obs, out = rest if weighted else (None, rest[0])
    shape = own.shape[1:]
    rightward = right_lanes(shape)
    blocks = []
    for p in range(outs):
        way, which = par[first + p, step], par[first + p, 4 + step]

        def pick(j):
            return jnp.where(way == 1, own[j], jnp.where(way == 0, north[j], south[j]))

        left = p - 1 if p > 0 else outs
        right = p + 1 if p < outs - 1 else outs
        edges = jnp.where(rightward, pick(right), pick(left))
        window = jnp.concatenate([pick(p), edges], axis=1)
        interp = jnp.dot(window, window_weights(table, which), preferred_element_type=F32).astype(BF16)
        mixed = jnp.dot(mix[step][:, : shape[0]], interp, preferred_element_type=F32).astype(BF16)
        if weighted:
            mixed = (obs[p].astype(F32) * mixed.astype(F32)).astype(BF16)
        if fold and p in (0, outs - 1):
            blocks.append(mixed)
        else:
            out[p - 1 if fold else p] = mixed
    if fold:
        out[outs - 2] = jnp.where(rightward, blocks[1], blocks[0])


def forward(step, outs, fold, par, rows, table, mix, obs=None):
    levels, cols = rows[0].shape[1:]
    first = (par.shape[0] - outs) // 2
    made = outs - 1 if fold else outs
    weighted = obs is not None
    args = (par, *rows, table, mix) + ((obs,) if weighted else ())
    return pl.pallas_call(
        functools.partial(forward_kernel, step, first, outs, fold, weighted),
        out_shape=jax.ShapeDtypeStruct((made, levels, cols), BF16),
        in_specs=[SMEM] + [VMEM] * (len(args) - 1),
        out_specs=VMEM,
        compiler_params=pltpu.CompilerParams(vmem_limit_bytes=LIMIT),
        cost_estimate=pl.CostEstimate(flops=outs * 6_000_000, bytes_accessed=2_000_000, transcendentals=0),
    )(*args)


def adjoint_kernel(step, first, reads, summed, par, *rest):
    parts, (table, mix, to_north, stay, to_south, total) = rest[: 3 if summed else 1], rest[3 if summed else 1 :]
    shape = parts[0].shape[1:]
    rightward = right_lanes(shape)
    nothing = jnp.zeros(shape, F32)
    for way in range(3):
        for p in range(reads):
            total[way, p] = nothing
    for p in range(reads):
        way, which = par[first + p, step], par[first + p, 4 + step]
        if summed:
            cot = (parts[0][p] + parts[1][p].astype(F32) + parts[2][p].astype(F32)).astype(BF16)
        else:
            cot = parts[0][p]
        back = lax.dot_general(mix[step][:, : shape[0]], cot, (((0,), (0,)), ((), ())), preferred_element_type=F32).astype(BF16)
        spread = lax.dot_general(back, window_weights(table, which), (((1,), (1,)), ((), ())), preferred_element_type=F32)
        main, edges = spread[:, : shape[1]], spread[:, shape[1] :]
        if 0 < p < reads - 1:
            total[way, p] += main
        if p < reads - 2:
            total[way, p + 1] += jnp.where(rightward, edges, nothing)
        if p > 1:
            total[way, p - 1] += jnp.where(rightward, nothing, edges)
    for p in range(1, reads - 1):
        to_north[p - 1] = total[0, p].astype(BF16)
        stay[p - 1] = total[1, p]
        to_south[p - 1] = total[2, p].astype(BF16)


def adjoint(step, par, parts, table, mix):
    reads, levels, cols = parts[0].shape
    first = (par.shape[0] - reads) // 2
    gives = (reads - 2, levels, cols)
    return pl.pallas_call(
        functools.partial(adjoint_kernel, step, first, reads, len(parts) == 3),
        out_shape=[jax.ShapeDtypeStruct(gives, BF16), jax.ShapeDtypeStruct(gives, F32), jax.ShapeDtypeStruct(gives, BF16)],
        in_specs=[SMEM] + [VMEM] * (len(parts) + 2),
        out_specs=[VMEM] * 3,
        scratch_shapes=[pltpu.VMEM((3, reads, levels, cols), F32)],
        compiler_params=pltpu.CompilerParams(vmem_limit_bytes=LIMIT),
        cost_estimate=pl.CostEstimate(flops=reads * 6_000_000, bytes_accessed=2_000_000, transcendentals=0),
    )(par, *parts, table, mix)


def homes():
    half, run = lax.axis_size("lat") // 2, 8
    rows, blocks = lax.axis_size("lat"), lax.axis_size("lon")

    def home(row, block):
        z, side = divmod(row, 2)
        column, slot = divmod(block, run)
        y, core = divmod(slot, 2)
        return (core * half + z) * blocks + column * run + y * 2 + side

    return rows, blocks, home


def move(value, pairs):
    return lax.ppermute(value, ("lat", "lon"), pairs)


def go_home(value, back=False):
    rows, blocks, home = homes()
    pairs = [(r * blocks + b, home(r, b)) for r in range(rows) for b in range(blocks)]
    return move(value, [(t, s) for s, t in pairs] if back else pairs)


def from_lat(value, by):
    rows, blocks, home = homes()
    return move(value, [(home(r, b), home(r - by, b)) for r in range(rows) for b in range(blocks) if 0 <= r - by < rows])


def from_lon(value, by):
    rows, blocks, home = homes()
    return move(value, [(home(r, b), home(r, (b - by) % blocks)) for r in range(rows) for b in range(blocks)])


def exchange(value, run):
    rows, blocks, home = homes()
    groups = [[home(r, b + j) for j in range(run)] for r in range(rows) for b in range(0, blocks, run)]
    return lax.all_to_all(value, ("lat", "lon"), 0, 0, axis_index_groups=groups)


def on_device(vector, obs_weight, departures, weight_index, interp_table, column_mix):
    run, levels, _, cols = vector.shape
    numbers = jnp.concatenate([departures.reshape(-1), weight_index.reshape(-1)]).astype(BF16)
    count = numbers.shape[0]
    tail = jnp.concatenate([jnp.broadcast_to(numbers[:, None], (count, cols)), jnp.zeros((16 - count, cols), BF16)])
    mix = jnp.pad(column_mix[:, 0], ((0, 0), (0, 0), (0, cols - levels)))
    steps = mix.shape[0]
    sent = jnp.concatenate([vector.reshape(-1, cols), mix.reshape(-1, cols), obs_weight[:, 0].astype(BF16), tail])
    sent = go_home(sent)
    mix = sent[run * levels : (run + steps) * levels].reshape(steps, levels, cols)
    shared = sent[(run + steps) * levels :]
    bundle = jnp.concatenate(
        [sent[: run * levels].reshape(run, levels, cols), jnp.broadcast_to(shared[None], (run, *shared.shape))], axis=1
    )
    bundle = exchange(bundle, run)
    state, obs = bundle[:, :levels], bundle[:, levels : 2 * levels]
    west, east = from_lon(bundle[-2:], -run), from_lon(bundle[:2], run)

    def read(part):
        return jnp.max(part[:, 2 * levels : 2 * levels + count].astype(F32), axis=2).astype(jnp.int32)

    par = jnp.concatenate([read(west), read(bundle), read(east)])
    west, east = west[:, :levels], east[:, :levels]

    for step in range(0, 4, 2):
        if step > 0:
            west, east = from_lon(state[-2:], -run), from_lon(state[:2], run)
        rightward = right_lanes((levels, cols))
        outer = jnp.where(rightward, east[1], west[0])
        wide = jnp.concatenate([west[1:], state, east[:1], outer[None]])
        wide = forward(step, run + 2, True, par, (wide, from_lat(wide, -1), from_lat(wide, 1)), interp_table, mix)
        state = forward(
            step + 1, run, False, par, (wide, from_lat(wide, -1), from_lat(wide, 1)), interp_table, mix,
            obs if step == 2 else None,
        )

    cot = state
    for step in (3, 1):
        west, east = from_lon(cot[-2:], -run), from_lon(cot[:2], run)
        wide = jnp.concatenate([west, cot, east])
        north, stay, south = adjoint(step, par, (wide,), interp_table, mix)
        parts = (stay, from_lat(north, 1), from_lat(south, -1))
        north, stay, south = adjoint(step - 1, par, parts, interp_table, mix)
        cot = (stay + from_lat(north, 1).astype(F32) + from_lat(south, -1).astype(F32)).astype(BF16)
    return go_home(exchange(cot, run), back=True)[:, :, None]


def solution(mesh):
    placed = (
        P(None, None, "lat", "lon"),
        P(None, "lat", "lon"),
        P(None, "lat", "lon"),
        P(None, "lat", "lon"),
        P(),
        P(None, "lat", None, None),
    )
    return jax.shard_map(
        on_device, mesh=mesh, in_specs=placed, out_specs=P(None, None, "lat", "lon"), check_vma=False
    )
```

```python
import functools

import jax
import jax.numpy as jnp
from jax import lax
from jax.experimental import pallas as pl
from jax.experimental.pallas import tpu as pltpu
from jax.sharding import PartitionSpec as P

F32, BF16 = jnp.float32, jnp.bfloat16
VMEM = pl.BlockSpec(memory_space=pltpu.VMEM)
SMEM = pl.BlockSpec(memory_space=pltpu.SMEM)
LIMIT = 24 * 1024 * 1024
RUN = 8


def right_lanes(shape):
    return lax.broadcasted_iota(jnp.int32, shape, 1) < shape[1] // 2


def window_weights(table, which):
    weights = table[which]
    cols = weights.shape[1]
    reach = (weights.shape[0] - cols) // 2
    gap = jnp.zeros((cols - 2 * reach, cols), weights.dtype)
    return jnp.concatenate([weights[reach : reach + cols], weights[reach + cols :], gap, weights[:reach]], axis=0)


def forward_kernel(step, first, outs, fold, weighted, par, own, north, south, table, mix, *rest):
    obs, out = rest if weighted else (None, rest[0])
    shape = own.shape[1:]
    rightward = right_lanes(shape)
    blocks = []
    for p in range(outs):
        way, which = par[first + p, step], par[first + p, 4 + step]

        def pick(j):
            return jnp.where(way == 1, own[j], jnp.where(way == 0, north[j], south[j]))

        left = p - 1 if p > 0 else outs
        right = p + 1 if p < outs - 1 else outs
        edges = jnp.where(rightward, pick(right), pick(left))
        window = jnp.concatenate([pick(p), edges], axis=1)
        interp = jnp.dot(window, window_weights(table, which), preferred_element_type=F32).astype(BF16)
        mixed = jnp.dot(mix[step][:, : shape[0]], interp, preferred_element_type=F32).astype(BF16)
        if weighted:
            mixed = (obs[p].astype(F32) * mixed.astype(F32)).astype(BF16)
        if fold and p in (0, outs - 1):
            blocks.append(mixed)
        else:
            out[p - 1 if fold else p] = mixed
    if fold:
        out[outs - 2] = jnp.where(rightward, blocks[1], blocks[0])


def forward(step, outs, fold, par, rows, table, mix, obs=None):
    levels, cols = rows[0].shape[1:]
    first = (par.shape[0] - outs) // 2
    made = outs - 1 if fold else outs
    weighted = obs is not None
    args = (par, *rows, table, mix) + ((obs,) if weighted else ())
    return pl.pallas_call(
        functools.partial(forward_kernel, step, first, outs, fold, weighted),
        out_shape=jax.ShapeDtypeStruct((made, levels, cols), BF16),
        in_specs=[SMEM] + [VMEM] * (len(args) - 1),
        out_specs=VMEM,
        compiler_params=pltpu.CompilerParams(vmem_limit_bytes=LIMIT),
        cost_estimate=pl.CostEstimate(flops=outs * 6_000_000, bytes_accessed=2_000_000, transcendentals=0),
    )(*args)


def adjoint_kernel(step, first, reads, summed, par, *rest):
    parts, (table, mix, to_north, stay, to_south, total) = rest[: 3 if summed else 1], rest[3 if summed else 1 :]
    shape = parts[0].shape[1:]
    rightward = right_lanes(shape)
    nothing = jnp.zeros(shape, F32)
    for way in range(3):
        for p in range(reads):
            total[way, p] = nothing
    for p in range(reads):
        way, which = par[first + p, step], par[first + p, 4 + step]
        if summed:
            cot = (parts[0][p] + parts[1][p].astype(F32) + parts[2][p].astype(F32)).astype(BF16)
        else:
            cot = parts[0][p]
        back = lax.dot_general(mix[step][:, : shape[0]], cot, (((0,), (0,)), ((), ())), preferred_element_type=F32).astype(BF16)
        spread = lax.dot_general(back, window_weights(table, which), (((1,), (1,)), ((), ())), preferred_element_type=F32)
        main, edges = spread[:, : shape[1]], spread[:, shape[1] :]
        if 0 < p < reads - 1:
            total[way, p] += main
        if p < reads - 2:
            total[way, p + 1] += jnp.where(rightward, edges, nothing)
        if p > 1:
            total[way, p - 1] += jnp.where(rightward, nothing, edges)
    for p in range(1, reads - 1):
        to_north[p - 1] = total[0, p].astype(BF16)
        stay[p - 1] = total[1, p]
        to_south[p - 1] = total[2, p].astype(BF16)


def adjoint(step, par, parts, table, mix):
    reads, levels, cols = parts[0].shape
    first = (par.shape[0] - reads) // 2
    gives = (reads - 2, levels, cols)
    return pl.pallas_call(
        functools.partial(adjoint_kernel, step, first, reads, len(parts) == 3),
        out_shape=[jax.ShapeDtypeStruct(gives, BF16), jax.ShapeDtypeStruct(gives, F32), jax.ShapeDtypeStruct(gives, BF16)],
        in_specs=[SMEM] + [VMEM] * (len(parts) + 2),
        out_specs=[VMEM] * 3,
        scratch_shapes=[pltpu.VMEM((3, reads, levels, cols), F32)],
        compiler_params=pltpu.CompilerParams(vmem_limit_bytes=LIMIT),
        cost_estimate=pl.CostEstimate(flops=reads * 6_000_000, bytes_accessed=2_000_000, transcendentals=0),
    )(par, *parts, table, mix)


def homes():
    rows, blocks = lax.axis_size("lat"), lax.axis_size("lon")

    def home(row, block):
        half, z = divmod(row, rows // 2)
        column, tracer = divmod(block, RUN)
        return place(rows, blocks, z, column, tracer, half)

    return rows, blocks, home


def place(rows, blocks, z, column, y, core):
    upper, y = divmod(y, RUN // 2)
    return (upper * (rows // 2) + z) * blocks + column * RUN + y * 2 + core


def move(value, pairs):
    return lax.ppermute(value, ("lat", "lon"), pairs)


def from_lat(value, by):
    rows, blocks, home = homes()
    return move(value, [(home(r, b), home(r - by, b)) for r in range(rows) for b in range(blocks) if 0 <= r - by < rows])


def from_lon(value, by):
    rows, blocks, home = homes()
    return move(value, [(home(r, b), home(r, (b - by) % blocks)) for r in range(rows) for b in range(blocks)])


def along_y(value):
    rows, blocks, _ = homes()
    groups = [
        [place(rows, blocks, z, column, y, core) for y in range(RUN)]
        for z in range(rows // 2)
        for column in range(blocks // RUN)
        for core in range(2)
    ]
    return lax.all_to_all(value, ("lat", "lon"), 0, 0, axis_index_groups=groups)


def swap_cores(value, first):
    keep, give = jnp.where(first, value[0], value[1]), jnp.where(first, value[1], value[0])
    blocks = lax.axis_size("lon")
    both = lax.all_gather(give, "lon", axis_index_groups=[[i, i + 1] for i in range(0, blocks, 2)])
    return jnp.where(first, keep, both[0]), jnp.where(first, both[1], keep)


def on_device(vector, obs_weight, departures, weight_index, interp_table, column_mix):
    run, levels, _, cols = vector.shape
    first = lax.axis_index("lon") % 2 == 0
    numbers = jnp.concatenate([departures.reshape(-1), weight_index.reshape(-1)]).astype(BF16)
    count = numbers.shape[0]
    tail = jnp.concatenate([jnp.broadcast_to(numbers[:, None], (count, cols)), jnp.zeros((16 - count, cols), BF16)])
    part = lax.dynamic_index_in_dim(column_mix[:, 0], lax.axis_index("lon") // 2 % column_mix.shape[0], keepdims=False)
    part = jnp.pad(part, ((0, 0), (0, cols - levels)))
    shared = jnp.concatenate([obs_weight[:, 0].astype(BF16), tail, part])
    bundle = along_y(
        jnp.concatenate([vector[:, :, 0], jnp.broadcast_to(shared[None], (run, *shared.shape))], axis=1)
    )
    bundle = bundle.reshape(2, run // 2, *bundle.shape[1:])
    mix = jnp.where(first, bundle[0, :, -levels:], bundle[1, :, -levels:])
    bundle = jnp.stack(swap_cores(bundle[:, :, :-levels], first), axis=1).reshape(run, -1, cols)
    state, obs = bundle[:, :levels], bundle[:, levels : 2 * levels]
    west, east = from_lon(bundle[-2:], -run), from_lon(bundle[:2], run)

    def read(part):
        return jnp.max(part[:, 2 * levels : 2 * levels + count].astype(F32), axis=2).astype(jnp.int32)

    par = jnp.concatenate([read(west), read(bundle), read(east)])
    west, east = west[:, :levels], east[:, :levels]

    for step in range(0, 4, 2):
        if step > 0:
            west, east = from_lon(state[-2:], -run), from_lon(state[:2], run)
        rightward = right_lanes((levels, cols))
        outer = jnp.where(rightward, east[1], west[0])
        wide = jnp.concatenate([west[1:], state, east[:1], outer[None]])
        wide = forward(step, run + 2, True, par, (wide, from_lat(wide, -1), from_lat(wide, 1)), interp_table, mix)
        state = forward(
            step + 1, run, False, par, (wide, from_lat(wide, -1), from_lat(wide, 1)), interp_table, mix,
            obs if step == 2 else None,
        )

    cot = state
    for step in (3, 1):
        west, east = from_lon(cot[-2:], -run), from_lon(cot[:2], run)
        wide = jnp.concatenate([west, cot, east])
        north, stay, south = adjoint(step, par, (wide,), interp_table, mix)
        parts = (stay, from_lat(north, 1), from_lat(south, -1))
        north, stay, south = adjoint(step - 1, par, parts, interp_table, mix)
        cot = (stay + from_lat(north, 1).astype(F32) + from_lat(south, -1).astype(F32)).astype(BF16)
    cot = cot.reshape(run // 2, 2, levels, cols)
    lower, upper = swap_cores((cot[:, 0], cot[:, 1]), first)
    return along_y(jnp.concatenate([lower, upper]))[:, :, None]


def solution(mesh):
    placed = (
        P(None, None, "lat", "lon"),
        P(None, "lat", "lon"),
        P(None, "lat", "lon"),
        P(None, "lat", "lon"),
        P(),
        P(None, "lat", None, None),
    )
    return jax.shard_map(
        on_device, mesh=mesh, in_specs=placed, out_specs=P(None, None, "lat", "lon"), check_vma=False
    )
```

```python
import functools

import jax
import jax.numpy as jnp
from jax import lax
from jax.experimental import pallas as pl
from jax.experimental.pallas import tpu as pltpu
from jax.sharding import PartitionSpec as P

F32, BF16 = jnp.float32, jnp.bfloat16
VMEM = pl.BlockSpec(memory_space=pltpu.VMEM)
SMEM = pl.BlockSpec(memory_space=pltpu.SMEM)
LIMIT = 24 * 1024 * 1024
RUN = 8


def right_lanes(shape):
    return lax.broadcasted_iota(jnp.int32, shape, 1) < shape[1] // 2


def window_weights(table, which):
    weights = table[which]
    cols = weights.shape[1]
    reach = (weights.shape[0] - cols) // 2
    gap = jnp.zeros((cols - 2 * reach, cols), weights.dtype)
    return jnp.concatenate([weights[reach : reach + cols], weights[reach + cols :], gap, weights[:reach]], axis=0)


def forward_kernel(step, first, outs, fold, weighted, par, own, north, south, table, mix, *rest):
    obs, out = rest if weighted else (None, rest[0])
    shape = own.shape[1:]
    rightward = right_lanes(shape)
    blocks = []
    for p in range(outs):
        way, which = par[first + p, step], par[first + p, 4 + step]

        def pick(j):
            return jnp.where(way == 1, own[j], jnp.where(way == 0, north[j], south[j]))

        left = p - 1 if p > 0 else outs
        right = p + 1 if p < outs - 1 else outs
        edges = jnp.where(rightward, pick(right), pick(left))
        window = jnp.concatenate([pick(p), edges], axis=1)
        interp = jnp.dot(window, window_weights(table, which), preferred_element_type=F32).astype(BF16)
        mixed = jnp.dot(mix[step][:, : shape[0]], interp, preferred_element_type=F32).astype(BF16)
        if weighted:
            mixed = (obs[p].astype(F32) * mixed.astype(F32)).astype(BF16)
        if fold and p in (0, outs - 1):
            blocks.append(mixed)
        else:
            out[p - 1 if fold else p] = mixed
    if fold:
        out[outs - 2] = jnp.where(rightward, blocks[1], blocks[0])


def forward(step, outs, fold, par, rows, table, mix, obs=None):
    levels, cols = rows[0].shape[1:]
    first = (par.shape[0] - outs) // 2
    made = outs - 1 if fold else outs
    weighted = obs is not None
    args = (par, *rows, table, mix) + ((obs,) if weighted else ())
    return pl.pallas_call(
        functools.partial(forward_kernel, step, first, outs, fold, weighted),
        out_shape=jax.ShapeDtypeStruct((made, levels, cols), BF16),
        in_specs=[SMEM] + [VMEM] * (len(args) - 1),
        out_specs=VMEM,
        compiler_params=pltpu.CompilerParams(vmem_limit_bytes=LIMIT),
        cost_estimate=pl.CostEstimate(flops=outs * 6_000_000, bytes_accessed=2_000_000, transcendentals=0),
    )(*args)


def adjoint_kernel(step, first, reads, summed, par, *rest):
    parts, (table, mix, to_north, stay, to_south, total) = rest[: 3 if summed else 1], rest[3 if summed else 1 :]
    shape = parts[0].shape[1:]
    rightward = right_lanes(shape)
    nothing = jnp.zeros(shape, F32)
    for way in range(3):
        for p in range(reads):
            total[way, p] = nothing
    for p in range(reads):
        way, which = par[first + p, step], par[first + p, 4 + step]
        if summed:
            cot = (parts[0][p] + parts[1][p].astype(F32) + parts[2][p].astype(F32)).astype(BF16)
        else:
            cot = parts[0][p]
        back = lax.dot_general(mix[step][:, : shape[0]], cot, (((0,), (0,)), ((), ())), preferred_element_type=F32).astype(BF16)
        spread = lax.dot_general(back, window_weights(table, which), (((1,), (1,)), ((), ())), preferred_element_type=F32)
        main, edges = spread[:, : shape[1]], spread[:, shape[1] :]
        if 0 < p < reads - 1:
            total[way, p] += main
        if p < reads - 2:
            total[way, p + 1] += jnp.where(rightward, edges, nothing)
        if p > 1:
            total[way, p - 1] += jnp.where(rightward, nothing, edges)
    for p in range(1, reads - 1):
        to_north[p - 1] = total[0, p].astype(BF16)
        stay[p - 1] = total[1, p]
        to_south[p - 1] = total[2, p].astype(BF16)


def adjoint(step, par, parts, table, mix):
    reads, levels, cols = parts[0].shape
    first = (par.shape[0] - reads) // 2
    gives = (reads - 2, levels, cols)
    return pl.pallas_call(
        functools.partial(adjoint_kernel, step, first, reads, len(parts) == 3),
        out_shape=[jax.ShapeDtypeStruct(gives, BF16), jax.ShapeDtypeStruct(gives, F32), jax.ShapeDtypeStruct(gives, BF16)],
        in_specs=[SMEM] + [VMEM] * (len(parts) + 2),
        out_specs=[VMEM] * 3,
        scratch_shapes=[pltpu.VMEM((3, reads, levels, cols), F32)],
        compiler_params=pltpu.CompilerParams(vmem_limit_bytes=LIMIT),
        cost_estimate=pl.CostEstimate(flops=reads * 6_000_000, bytes_accessed=2_000_000, transcendentals=0),
    )(par, *parts, table, mix)


def homes():
    rows, blocks = lax.axis_size("lat"), lax.axis_size("lon")

    def home(row, block):
        half, z = divmod(row, rows // 2)
        column, tracer = divmod(block, RUN)
        return place(rows, blocks, z, column, tracer, half)

    return rows, blocks, home


def place(rows, blocks, z, column, y, core):
    upper, y = divmod(y, RUN // 2)
    return (upper * (rows // 2) + z) * blocks + column * RUN + y * 2 + core


def move(value, pairs):
    return lax.ppermute(value, ("lat", "lon"), pairs)


def from_lat(value, by):
    rows, blocks, home = homes()
    return move(value, [(home(r, b), home(r - by, b)) for r in range(rows) for b in range(blocks) if 0 <= r - by < rows])


def from_lon(value, by):
    rows, blocks, home = homes()
    return move(value, [(home(r, b), home(r, (b - by) % blocks)) for r in range(rows) for b in range(blocks)])


def along_y(value):
    rows, blocks, _ = homes()
    groups = [
        [place(rows, blocks, z, column, y, core) for y in range(RUN)]
        for z in range(rows // 2)
        for column in range(blocks // RUN)
        for core in range(2)
    ]
    return lax.all_to_all(value, ("lat", "lon"), 0, 0, axis_index_groups=groups)


def swap_cores(value, first):
    keep, give = jnp.where(first, value[0], value[1]), jnp.where(first, value[1], value[0])
    blocks = lax.axis_size("lon")
    both = lax.all_gather(give, "lon", axis_index_groups=[[i, i + 1] for i in range(0, blocks, 2)])
    return jnp.where(first, keep, both[0]), jnp.where(first, both[1], keep)


def on_device(vector, obs_weight, departures, weight_index, interp_table, column_mix):
    run, levels, _, cols = vector.shape
    first = lax.axis_index("lon") % 2 == 0
    numbers = jnp.concatenate([departures.reshape(-1), weight_index.reshape(-1)]).astype(BF16)
    count = numbers.shape[0]
    tail = jnp.concatenate([jnp.broadcast_to(numbers[:, None], (count, cols)), jnp.zeros((16 - count, cols), BF16)])
    part = lax.dynamic_index_in_dim(column_mix[:, 0], lax.axis_index("lon") // 2 % column_mix.shape[0], keepdims=False)
    part = jnp.pad(part, ((0, 0), (0, cols - levels)))
    shared = jnp.concatenate([tail, obs_weight[:, 0].astype(BF16), part])
    bundle = along_y(
        jnp.concatenate([vector[:, :, 0], jnp.broadcast_to(shared[None], (run, *shared.shape))], axis=1)
    )
    bundle = bundle.reshape(2, run // 2, *bundle.shape[1:])
    mix = jnp.where(first, bundle[0, :, -levels:], bundle[1, :, -levels:])
    bundle = jnp.stack(swap_cores(bundle[:, :, :-levels], first), axis=1).reshape(run, -1, cols)
    marked = levels + tail.shape[0]
    state, obs = bundle[:, :levels], bundle[:, marked:]
    reach = column_mix.shape[0]
    west, east = from_lon(bundle[-reach:, :marked], -run), from_lon(bundle[:reach, :marked], run)

    def read(part):
        return jnp.max(part[:, levels : levels + count].astype(F32), axis=2).astype(jnp.int32)

    par = jnp.concatenate([read(west), read(bundle), read(east)])
    outer = jnp.where(right_lanes((levels, cols)), east[-1, :levels], west[0, :levels])
    state = jnp.concatenate([west[1:, :levels], state, east[:-1, :levels], outer[None]])
    for step in range(reach):
        last = step == reach - 1
        rows = (state, from_lat(state, -1), from_lat(state, 1))
        state = forward(step, run + 2 * (reach - 1 - step), not last, par, rows, interp_table, mix, obs if last else None)

    west, east = from_lon(state[-reach:], -run), from_lon(state[:reach], run)
    parts = (jnp.concatenate([west, state, east]),)
    for step in reversed(range(reach)):
        north, stay, south = adjoint(step, par, parts, interp_table, mix)
        parts = (stay, from_lat(north, 1), from_lat(south, -1))
    cot = sum(part.astype(F32) for part in parts).astype(BF16)
    cot = cot.reshape(run // 2, 2, levels, cols)
    lower, upper = swap_cores((cot[:, 0], cot[:, 1]), first)
    return along_y(jnp.concatenate([lower, upper]))[:, :, None]


def solution(mesh):
    placed = (
        P(None, None, "lat", "lon"),
        P(None, "lat", "lon"),
        P(None, "lat", "lon"),
        P(None, "lat", "lon"),
        P(),
        P(None, "lat", None, None),
    )
    return jax.shard_map(
        on_device, mesh=mesh, in_specs=placed, out_specs=P(None, None, "lat", "lon"), check_vma=False
    )
```

```python
import functools

import jax
import jax.numpy as jnp
from jax import lax
from jax.experimental import pallas as pl
from jax.experimental.pallas import tpu as pltpu
from jax.sharding import PartitionSpec as P

F32, BF16 = jnp.float32, jnp.bfloat16
VMEM = pl.BlockSpec(memory_space=pltpu.VMEM)
SMEM = pl.BlockSpec(memory_space=pltpu.SMEM)
LIMIT = 24 * 1024 * 1024
RUN = 8


def right_lanes(shape):
    return lax.broadcasted_iota(jnp.int32, shape, 1) < shape[1] // 2


def window_weights(weights):
    cols = weights.shape[1]
    reach = (weights.shape[0] - cols) // 2
    gap = jnp.zeros((cols - 2 * reach, cols), weights.dtype)
    return jnp.concatenate([weights[reach : reach + cols], weights[reach + cols :], gap, weights[:reach]], axis=0)


def turn_kernel(table, out):
    for i in range(table.shape[0]):
        out[i] = window_weights(table[i]).astype(F32).T.astype(BF16)


def turn(table):
    count, _, cols = table.shape
    return pl.pallas_call(
        turn_kernel,
        out_shape=jax.ShapeDtypeStruct((count, cols, 2 * cols), BF16),
        in_specs=[VMEM],
        out_specs=VMEM,
        compiler_params=pltpu.CompilerParams(vmem_limit_bytes=LIMIT),
        cost_estimate=pl.CostEstimate(flops=0, bytes_accessed=6_000_000, transcendentals=0),
    )(table)


def choose_kernel(outside, par, table, out):
    steps, blocks = out.shape[:2]
    for step in range(steps):
        for p in range(outside(step), blocks - outside(step)):
            out[step, p] = table[par[p, steps + step]]


def choose(par, table, steps, outside):
    return pl.pallas_call(
        functools.partial(choose_kernel, outside),
        out_shape=jax.ShapeDtypeStruct((steps, par.shape[0], *table.shape[1:]), BF16),
        in_specs=[SMEM, VMEM],
        out_specs=VMEM,
        compiler_params=pltpu.CompilerParams(vmem_limit_bytes=LIMIT),
        cost_estimate=pl.CostEstimate(flops=0, bytes_accessed=6_000_000, transcendentals=0),
    )(par, table)


def forward_kernel(step, first, outs, fold, weighted, marks, own, north, south, weights, mix, *rest):
    obs, out = rest if weighted else (None, rest[0])
    shape = own.shape[1:]
    rightward = right_lanes(shape)
    mixing = mix[step][:, : shape[0]]
    blocks = []
    for p in range(outs):
        way = jnp.broadcast_to(marks[first + p][step : step + 1].astype(F32), shape)
        stay, up = way == 1, way == 0

        def pick(j):
            return jnp.where(stay, own[j], jnp.where(up, north[j], south[j]))

        left = p - 1 if p > 0 else outs
        right = p + 1 if p < outs - 1 else outs
        edges = jnp.where(rightward, pick(right), pick(left))
        window = jnp.concatenate([pick(p), edges], axis=1)
        interp = jnp.dot(window, window_weights(weights[step, first + p]), preferred_element_type=F32).astype(BF16)
        mixed = jnp.dot(mixing, interp, preferred_element_type=F32).astype(BF16)
        if weighted:
            mixed = (obs[p].astype(F32) * mixed.astype(F32)).astype(BF16)
        if fold and p in (0, outs - 1):
            blocks.append(mixed)
        else:
            out[p - 1 if fold else p] = mixed
    if fold:
        out[outs - 2] = jnp.where(rightward, blocks[1], blocks[0])


def forward(step, outs, fold, marks, rows, weights, mix, obs=None):
    levels, cols = rows[0].shape[1:]
    first = (marks.shape[0] - outs) // 2
    made = outs - 1 if fold else outs
    weighted = obs is not None
    args = (marks, *rows, weights, mix) + ((obs,) if weighted else ())
    return pl.pallas_call(
        functools.partial(forward_kernel, step, first, outs, fold, weighted),
        out_shape=jax.ShapeDtypeStruct((made, levels, cols), BF16),
        in_specs=[VMEM] * len(args),
        out_specs=VMEM,
        compiler_params=pltpu.CompilerParams(vmem_limit_bytes=LIMIT),
        cost_estimate=pl.CostEstimate(flops=outs * 6_000_000, bytes_accessed=2_000_000, transcendentals=0),
    )(*args)


def adjoint_kernel(step, first, reads, summed, marks, *rest):
    parts, (weights, mix, to_north, stay, to_south, spreads) = rest[: 3 if summed else 1], rest[3 if summed else 1 :]
    shape = parts[0].shape[1:]
    cols = shape[1]
    rightward = right_lanes(shape)
    mixing = mix[step].astype(F32).T[: shape[0]].astype(BF16)
    for p in range(reads):
        if summed:
            cot = (parts[0][p] + parts[1][p].astype(F32) + parts[2][p].astype(F32)).astype(BF16)
        else:
            cot = parts[0][p]
        back = jnp.dot(mixing, cot, preferred_element_type=F32).astype(BF16)
        spreads[p] = jnp.dot(back, weights[step, first + p], preferred_element_type=F32)
    nothing = jnp.zeros(shape, F32)

    def way(p):
        return jnp.broadcast_to(marks[first + p][step : step + 1].astype(F32), shape)

    for p in range(1, reads - 1):
        main, to = spreads[p, :, :cols], way(p)
        edges = jnp.where(rightward, spreads[p - 1, :, cols:], spreads[p + 1, :, cols:])
        edges_to = jnp.where(rightward, way(p - 1), way(p + 1))
        total = [jnp.where(to == i, main, nothing) + jnp.where(edges_to == i, edges, nothing) for i in range(3)]
        to_north[p - 1] = total[0].astype(BF16)
        stay[p - 1] = total[1]
        to_south[p - 1] = total[2].astype(BF16)


def adjoint(step, marks, parts, weights, mix):
    reads, levels, cols = parts[0].shape
    first = (marks.shape[0] - reads) // 2
    gives = (reads - 2, levels, cols)
    return pl.pallas_call(
        functools.partial(adjoint_kernel, step, first, reads, len(parts) == 3),
        out_shape=[jax.ShapeDtypeStruct(gives, BF16), jax.ShapeDtypeStruct(gives, F32), jax.ShapeDtypeStruct(gives, BF16)],
        in_specs=[VMEM] * (len(parts) + 3),
        out_specs=[VMEM] * 3,
        scratch_shapes=[pltpu.VMEM((reads, levels, 2 * cols), F32)],
        compiler_params=pltpu.CompilerParams(vmem_limit_bytes=LIMIT),
        cost_estimate=pl.CostEstimate(flops=reads * 6_000_000, bytes_accessed=2_000_000, transcendentals=0),
    )(marks, *parts, weights, mix)


def homes():
    rows, blocks = lax.axis_size("lat"), lax.axis_size("lon")

    def home(row, block):
        half, z = divmod(row, rows // 2)
        column, tracer = divmod(block, RUN)
        return place(rows, blocks, z, column, tracer, half)

    return rows, blocks, home


def place(rows, blocks, z, column, y, core):
    upper, y = divmod(y, RUN // 2)
    return (upper * (rows // 2) + z) * blocks + column * RUN + y * 2 + core


def move(value, pairs):
    return lax.ppermute(value, ("lat", "lon"), pairs)


def from_lat(value, by):
    rows, blocks, home = homes()
    return move(value, [(home(r, b), home(r - by, b)) for r in range(rows) for b in range(blocks) if 0 <= r - by < rows])


def from_lon(value, by):
    rows, blocks, home = homes()
    return move(value, [(home(r, b), home(r, (b - by) % blocks)) for r in range(rows) for b in range(blocks)])


def along_y(value):
    rows, blocks, _ = homes()
    groups = [
        [place(rows, blocks, z, column, y, core) for y in range(RUN)]
        for z in range(rows // 2)
        for column in range(blocks // RUN)
        for core in range(2)
    ]
    return lax.all_to_all(value, ("lat", "lon"), 0, 0, axis_index_groups=groups)


def swap_cores(value, first):
    keep, give = jnp.where(first, value[0], value[1]), jnp.where(first, value[1], value[0])
    blocks = lax.axis_size("lon")
    both = lax.all_gather(give, "lon", axis_index_groups=[[i, i + 1] for i in range(0, blocks, 2)])
    return jnp.where(first, keep, both[0]), jnp.where(first, both[1], keep)


def on_device(vector, obs_weight, departures, weight_index, interp_table, column_mix):
    run, levels, _, cols = vector.shape
    first = lax.axis_index("lon") % 2 == 0
    numbers = jnp.concatenate([departures.reshape(-1), weight_index.reshape(-1)]).astype(BF16)
    count = numbers.shape[0]
    tail = jnp.broadcast_to(numbers[:, None], (count, cols))
    part = lax.dynamic_index_in_dim(column_mix[:, 0], lax.axis_index("lon") // 2 % column_mix.shape[0], keepdims=False)
    part = jnp.pad(part, ((0, 0), (0, cols - levels)))
    shared = jnp.concatenate([tail, obs_weight[:, 0].astype(BF16), part])
    bundle = along_y(
        jnp.concatenate([vector[:, :, 0], jnp.broadcast_to(shared[None], (run, *shared.shape))], axis=1)
    )
    bundle = bundle.reshape(2, run // 2, *bundle.shape[1:])
    mix = jnp.where(first, bundle[0, :, -levels:], bundle[1, :, -levels:])
    bundle = jnp.stack(swap_cores(bundle[:, :, :-levels], first), axis=1).reshape(run, -1, cols)
    marked = levels + count
    state, obs = bundle[:, :levels], bundle[:, marked:]
    reach = column_mix.shape[0]
    west, east = from_lon(bundle[-reach:, :marked], -run), from_lon(bundle[:reach, :marked], run)

    marks = jnp.concatenate([part[:, levels:marked] for part in (west, bundle, east)])
    par = jnp.max(marks.astype(F32), axis=2).astype(jnp.int32)
    weights = choose(par, interp_table, reach, lambda step: 1 + step)
    turned = choose(par, turn(interp_table), reach, lambda step: reach - 1 - step)
    outer = jnp.where(right_lanes((levels, cols)), east[-1, :levels], west[0, :levels])
    state = jnp.concatenate([west[1:, :levels], state, east[:-1, :levels], outer[None]])
    for step in range(reach):
        last = step == reach - 1
        rows = (state, from_lat(state, -1), from_lat(state, 1))
        state = forward(step, run + 2 * (reach - 1 - step), not last, marks, rows, weights, mix, obs if last else None)

    west, east = from_lon(state[-reach:], -run), from_lon(state[:reach], run)
    parts = (jnp.concatenate([west, state, east]),)
    for step in reversed(range(reach)):
        north, stay, south = adjoint(step, marks, parts, turned, mix)
        parts = (stay, from_lat(north, 1), from_lat(south, -1))
    cot = sum(part.astype(F32) for part in parts).astype(BF16)
    cot = cot.reshape(run // 2, 2, levels, cols)
    lower, upper = swap_cores((cot[:, 0], cot[:, 1]), first)
    return along_y(jnp.concatenate([lower, upper]))[:, :, None]


def solution(mesh):
    placed = (
        P(None, None, "lat", "lon"),
        P(None, "lat", "lon"),
        P(None, "lat", "lon"),
        P(None, "lat", "lon"),
        P(),
        P(None, "lat", None, None),
    )
    return jax.shard_map(
        on_device, mesh=mesh, in_specs=placed, out_specs=P(None, None, "lat", "lon"), check_vma=False
    )
```

```python
import functools

import jax
import jax.numpy as jnp
from jax import lax
from jax.experimental import pallas as pl
from jax.experimental.pallas import tpu as pltpu
from jax.sharding import PartitionSpec as P

F32, BF16 = jnp.float32, jnp.bfloat16
VMEM = pl.BlockSpec(memory_space=pltpu.VMEM)
SMEM = pl.BlockSpec(memory_space=pltpu.SMEM)
LIMIT = 24 * 1024 * 1024
RUN = 8


def right_lanes(shape):
    return lax.broadcasted_iota(jnp.int32, shape, 1) < shape[1] // 2


def bundle_kernel(mine, *refs):
    given, out, held, done = refs[:5], refs[5], refs[6:11], refs[11]
    copies = [pltpu.make_async_copy(given[i], held[i], done.at[i]) for i in range(5)]
    for copy in copies:
        copy.start()
    for copy in copies:
        copy.wait()
    departures, weight_index, vector, obs, mix = held
    run, levels, cols = vector.shape
    marks = [jnp.full((1, cols), ref[i]) for ref in (departures, weight_index) for i in range(ref.shape[0])]
    part = mix[mine[0]].astype(F32)
    part = jnp.concatenate([part, jnp.zeros((levels, cols - levels), F32)], axis=1)
    shared = jnp.concatenate([jnp.concatenate(marks).astype(F32), obs[...], part])
    for tracer in range(run):
        out[tracer] = jnp.concatenate([vector[tracer].astype(F32), shared]).astype(BF16)


def bundled(mine, departures, weight_index, vector, obs, mix):
    run, levels, cols = vector.shape
    rows = 3 * levels + departures.shape[0] + weight_index.shape[0]
    spaces = (pltpu.SMEM, pltpu.SMEM, pltpu.VMEM, pltpu.VMEM, pltpu.VMEM)
    given = (departures, weight_index, vector, obs, mix)
    return pl.pallas_call(
        bundle_kernel,
        out_shape=jax.ShapeDtypeStruct((run, rows, cols), BF16),
        in_specs=[SMEM] + [pl.BlockSpec(memory_space=pltpu.HBM)] * 5,
        out_specs=VMEM,
        scratch_shapes=[space(x.shape, x.dtype) for space, x in zip(spaces, given)] + [pltpu.SemaphoreType.DMA((5,))],
        compiler_params=pltpu.CompilerParams(vmem_limit_bytes=60 * 1024 * 1024),
        cost_estimate=pl.CostEstimate(flops=0, bytes_accessed=1_000_000, transcendentals=0),
    )(mine, *given)


def window_weights(weights):
    cols = weights.shape[1]
    reach = (weights.shape[0] - cols) // 2
    gap = jnp.zeros((cols - 2 * reach, cols), weights.dtype)
    return jnp.concatenate([weights[reach : reach + cols], weights[reach + cols :], gap, weights[:reach]], axis=0)


def turn_kernel(table, out):
    for i in range(table.shape[0]):
        out[i] = window_weights(table[i]).astype(F32).T.astype(BF16)


def turn(table):
    count, _, cols = table.shape
    return pl.pallas_call(
        turn_kernel,
        out_shape=jax.ShapeDtypeStruct((count, cols, 2 * cols), BF16),
        in_specs=[VMEM],
        out_specs=VMEM,
        compiler_params=pltpu.CompilerParams(vmem_limit_bytes=LIMIT),
        cost_estimate=pl.CostEstimate(flops=0, bytes_accessed=6_000_000, transcendentals=0),
    )(table)


def choose_kernel(outside, par, table, out):
    steps, blocks = out.shape[:2]
    for step in range(steps):
        for p in range(outside(step), blocks - outside(step)):
            out[step, p] = table[par[p, steps + step]]


def choose(par, table, steps, outside):
    return pl.pallas_call(
        functools.partial(choose_kernel, outside),
        out_shape=jax.ShapeDtypeStruct((steps, par.shape[0], *table.shape[1:]), BF16),
        in_specs=[SMEM, VMEM],
        out_specs=VMEM,
        compiler_params=pltpu.CompilerParams(vmem_limit_bytes=LIMIT),
        cost_estimate=pl.CostEstimate(flops=0, bytes_accessed=6_000_000, transcendentals=0),
    )(par, table)


def forward_kernel(step, first, outs, fold, weighted, marks, own, north, south, weights, mix, *rest):
    obs, out = rest if weighted else (None, rest[0])
    shape = own.shape[1:]
    rightward = right_lanes(shape)
    mixing = mix[step][:, : shape[0]]
    blocks = []
    for p in range(outs):
        way = jnp.broadcast_to(marks[first + p][step : step + 1].astype(F32), shape)
        stay, up = way == 1, way == 0

        def pick(j):
            return jnp.where(stay, own[j], jnp.where(up, north[j], south[j]))

        left = p - 1 if p > 0 else outs
        right = p + 1 if p < outs - 1 else outs
        edges = jnp.where(rightward, pick(right), pick(left))
        window = jnp.concatenate([pick(p), edges], axis=1)
        interp = jnp.dot(window, window_weights(weights[step, first + p]), preferred_element_type=F32).astype(BF16)
        mixed = jnp.dot(mixing, interp, preferred_element_type=F32).astype(BF16)
        if weighted:
            mixed = (obs[p].astype(F32) * mixed.astype(F32)).astype(BF16)
        if fold and p in (0, outs - 1):
            blocks.append(mixed)
        else:
            out[p - 1 if fold else p] = mixed
    if fold:
        out[outs - 2] = jnp.where(rightward, blocks[1], blocks[0])


def forward(step, outs, fold, marks, rows, weights, mix, obs=None):
    levels, cols = rows[0].shape[1:]
    first = (marks.shape[0] - outs) // 2
    made = outs - 1 if fold else outs
    weighted = obs is not None
    args = (marks, *rows, weights, mix) + ((obs,) if weighted else ())
    return pl.pallas_call(
        functools.partial(forward_kernel, step, first, outs, fold, weighted),
        out_shape=jax.ShapeDtypeStruct((made, levels, cols), BF16),
        in_specs=[VMEM] * len(args),
        out_specs=VMEM,
        compiler_params=pltpu.CompilerParams(vmem_limit_bytes=LIMIT),
        cost_estimate=pl.CostEstimate(flops=outs * 6_000_000, bytes_accessed=2_000_000, transcendentals=0),
    )(*args)


def adjoint_kernel(step, first, reads, summed, marks, *rest):
    parts, (weights, mix, to_north, stay, to_south, spreads) = rest[: 3 if summed else 1], rest[3 if summed else 1 :]
    shape = parts[0].shape[1:]
    cols = shape[1]
    rightward = right_lanes(shape)
    mixing = mix[step].astype(F32).T[: shape[0]].astype(BF16)
    for p in range(reads):
        if summed:
            cot = (parts[0][p] + parts[1][p].astype(F32) + parts[2][p].astype(F32)).astype(BF16)
        else:
            cot = parts[0][p]
        back = jnp.dot(mixing, cot, preferred_element_type=F32).astype(BF16)
        spreads[p] = jnp.dot(back, weights[step, first + p], preferred_element_type=F32)
    nothing = jnp.zeros(shape, F32)

    def way(p):
        return jnp.broadcast_to(marks[first + p][step : step + 1].astype(F32), shape)

    for p in range(1, reads - 1):
        main, to = spreads[p, :, :cols], way(p)
        edges = jnp.where(rightward, spreads[p - 1, :, cols:], spreads[p + 1, :, cols:])
        edges_to = jnp.where(rightward, way(p - 1), way(p + 1))
        total = [jnp.where(to == i, main, nothing) + jnp.where(edges_to == i, edges, nothing) for i in range(3)]
        to_north[p - 1] = total[0].astype(BF16)
        stay[p - 1] = total[1]
        to_south[p - 1] = total[2].astype(BF16)


def adjoint(step, marks, parts, weights, mix):
    reads, levels, cols = parts[0].shape
    first = (marks.shape[0] - reads) // 2
    gives = (reads - 2, levels, cols)
    return pl.pallas_call(
        functools.partial(adjoint_kernel, step, first, reads, len(parts) == 3),
        out_shape=[jax.ShapeDtypeStruct(gives, BF16), jax.ShapeDtypeStruct(gives, F32), jax.ShapeDtypeStruct(gives, BF16)],
        in_specs=[VMEM] * (len(parts) + 3),
        out_specs=[VMEM] * 3,
        scratch_shapes=[pltpu.VMEM((reads, levels, 2 * cols), F32)],
        compiler_params=pltpu.CompilerParams(vmem_limit_bytes=LIMIT),
        cost_estimate=pl.CostEstimate(flops=reads * 6_000_000, bytes_accessed=2_000_000, transcendentals=0),
    )(marks, *parts, weights, mix)


def homes():
    rows, blocks = lax.axis_size("lat"), lax.axis_size("lon")

    def home(row, block):
        half, z = divmod(row, rows // 2)
        column, tracer = divmod(block, RUN)
        return place(rows, blocks, z, column, tracer, half)

    return rows, blocks, home


def place(rows, blocks, z, column, y, core):
    upper, y = divmod(y, RUN // 2)
    return (upper * (rows // 2) + z) * blocks + column * RUN + y * 2 + core


def move(value, pairs):
    return lax.ppermute(value, ("lat", "lon"), pairs)


def from_lat(value, by):
    rows, blocks, home = homes()
    return move(value, [(home(r, b), home(r - by, b)) for r in range(rows) for b in range(blocks) if 0 <= r - by < rows])


def from_lon(value, by):
    rows, blocks, home = homes()
    return move(value, [(home(r, b), home(r, (b - by) % blocks)) for r in range(rows) for b in range(blocks)])


def along_y(value):
    rows, blocks, _ = homes()
    groups = [
        [place(rows, blocks, z, column, y, core) for y in range(RUN)]
        for z in range(rows // 2)
        for column in range(blocks // RUN)
        for core in range(2)
    ]
    return lax.all_to_all(value, ("lat", "lon"), 0, 0, axis_index_groups=groups)


def swap_cores(value, first):
    keep, give = jnp.where(first, value[0], value[1]), jnp.where(first, value[1], value[0])
    blocks = lax.axis_size("lon")
    both = lax.all_gather(give, "lon", axis_index_groups=[[i, i + 1] for i in range(0, blocks, 2)])
    return jnp.where(first, keep, both[0]), jnp.where(first, both[1], keep)


def on_device(vector, obs_weight, departures, weight_index, interp_table, column_mix):
    run, levels, _, cols = vector.shape
    first = lax.axis_index("lon") % 2 == 0
    steps = column_mix.shape[0]
    count = 2 * steps
    mine = (lax.axis_index("lon") // 2 % steps).reshape(1).astype(jnp.int32)
    bundle = along_y(
        bundled(
            mine, departures.reshape(-1), weight_index.reshape(-1), vector[:, :, 0], obs_weight[:, 0], column_mix[:, 0]
        )
    )
    bundle = bundle.reshape(2, run // 2, *bundle.shape[1:])
    mix = jnp.where(first, bundle[0, :, -levels:], bundle[1, :, -levels:])
    bundle = jnp.stack(swap_cores(bundle[:, :, :-levels], first), axis=1).reshape(run, -1, cols)
    marked = levels + count
    state, obs = bundle[:, :levels], bundle[:, marked:]
    reach = steps
    west, east = from_lon(bundle[-reach:, :marked], -run), from_lon(bundle[:reach, :marked], run)

    marks = jnp.concatenate([part[:, levels:marked] for part in (west, bundle, east)])
    par = jnp.max(marks.astype(F32), axis=2).astype(jnp.int32)
    weights = choose(par, interp_table, reach, lambda step: 1 + step)
    turned = choose(par, turn(interp_table), reach, lambda step: reach - 1 - step)
    outer = jnp.where(right_lanes((levels, cols)), east[-1, :levels], west[0, :levels])
    state = jnp.concatenate([west[1:, :levels], state, east[:-1, :levels], outer[None]])
    for step in range(reach):
        last = step == reach - 1
        rows = (state, from_lat(state, -1), from_lat(state, 1))
        state = forward(step, run + 2 * (reach - 1 - step), not last, marks, rows, weights, mix, obs if last else None)

    west, east = from_lon(state[-reach:], -run), from_lon(state[:reach], run)
    parts = (jnp.concatenate([west, state, east]),)
    for step in reversed(range(reach)):
        north, stay, south = adjoint(step, marks, parts, turned, mix)
        parts = (stay, from_lat(north, 1), from_lat(south, -1))
    cot = sum(part.astype(F32) for part in parts).astype(BF16)
    cot = cot.reshape(run // 2, 2, levels, cols)
    lower, upper = swap_cores((cot[:, 0], cot[:, 1]), first)
    return along_y(jnp.concatenate([lower, upper]))[:, :, None]


def solution(mesh):
    placed = (
        P(None, None, "lat", "lon"),
        P(None, "lat", "lon"),
        P(None, "lat", "lon"),
        P(None, "lat", "lon"),
        P(),
        P(None, "lat", None, None),
    )
    return jax.shard_map(
        on_device, mesh=mesh, in_specs=placed, out_specs=P(None, None, "lat", "lon"), check_vma=False
    )
```

```python
import functools

import jax
import jax.numpy as jnp
from jax import lax
from jax.experimental import pallas as pl
from jax.experimental.pallas import tpu as pltpu
from jax.sharding import PartitionSpec as P

F32, BF16 = jnp.float32, jnp.bfloat16
VMEM = pl.BlockSpec(memory_space=pltpu.VMEM)
SMEM = pl.BlockSpec(memory_space=pltpu.SMEM)
LIMIT = 24 * 1024 * 1024
RUN = 8


def right_lanes(shape):
    return lax.broadcasted_iota(jnp.int32, shape, 1) < shape[1] // 2


def bundle_kernel(mine, *refs):
    given, out, held, done = refs[:5], refs[5], refs[6:11], refs[11]
    copies = [pltpu.make_async_copy(given[i], held[i], done.at[i]) for i in range(5)]
    for copy in copies:
        copy.start()
    for copy in copies:
        copy.wait()
    departures, weight_index, vector, obs, mix = held
    run, levels, cols = vector.shape
    marks = [jnp.full((1, cols), ref[i]) for ref in (departures, weight_index) for i in range(ref.shape[0])]
    part = mix[mine[0] >> 1].astype(F32)
    share = out.shape[1] - 2 * levels - len(marks)
    part = jnp.where((mine[0] & 1) == 0, part[:share], part[levels - share :])
    part = jnp.concatenate([part, jnp.zeros((share, cols - levels), F32)], axis=1)
    shared = jnp.concatenate([jnp.concatenate(marks).astype(F32), obs[...], part])
    for tracer in range(run):
        out[tracer] = jnp.concatenate([vector[tracer].astype(F32), shared]).astype(BF16)


def bundled(mine, share, departures, weight_index, vector, obs, mix):
    run, levels, cols = vector.shape
    rows = 2 * levels + departures.shape[0] + weight_index.shape[0] + share
    spaces = (pltpu.SMEM, pltpu.SMEM, pltpu.VMEM, pltpu.VMEM, pltpu.VMEM)
    given = (departures, weight_index, vector, obs, mix)
    return pl.pallas_call(
        bundle_kernel,
        out_shape=jax.ShapeDtypeStruct((run, rows, cols), BF16),
        in_specs=[SMEM] + [pl.BlockSpec(memory_space=pltpu.HBM)] * 5,
        out_specs=VMEM,
        scratch_shapes=[space(x.shape, x.dtype) for space, x in zip(spaces, given)] + [pltpu.SemaphoreType.DMA((5,))],
        compiler_params=pltpu.CompilerParams(vmem_limit_bytes=60 * 1024 * 1024),
        cost_estimate=pl.CostEstimate(flops=0, bytes_accessed=1_000_000, transcendentals=0),
    )(mine, *given)


def window_weights(weights):
    cols = weights.shape[1]
    reach = (weights.shape[0] - cols) // 2
    gap = jnp.zeros((cols - 2 * reach, cols), weights.dtype)
    return jnp.concatenate([weights[reach : reach + cols], weights[reach + cols :], gap, weights[:reach]], axis=0)


def turn_kernel(table, out):
    for i in range(table.shape[0]):
        out[i] = window_weights(table[i]).astype(F32).T.astype(BF16)


def turn(table):
    count, _, cols = table.shape
    return pl.pallas_call(
        turn_kernel,
        out_shape=jax.ShapeDtypeStruct((count, cols, 2 * cols), BF16),
        in_specs=[VMEM],
        out_specs=VMEM,
        compiler_params=pltpu.CompilerParams(vmem_limit_bytes=LIMIT),
        cost_estimate=pl.CostEstimate(flops=0, bytes_accessed=6_000_000, transcendentals=0),
    )(table)


def choose_kernel(outside, par, table, out):
    steps, blocks = out.shape[:2]
    for step in range(steps):
        for p in range(outside(step), blocks - outside(step)):
            out[step, p] = table[par[p, steps + step]]


def choose(par, table, steps, outside):
    return pl.pallas_call(
        functools.partial(choose_kernel, outside),
        out_shape=jax.ShapeDtypeStruct((steps, par.shape[0], *table.shape[1:]), BF16),
        in_specs=[SMEM, VMEM],
        out_specs=VMEM,
        compiler_params=pltpu.CompilerParams(vmem_limit_bytes=LIMIT),
        cost_estimate=pl.CostEstimate(flops=0, bytes_accessed=6_000_000, transcendentals=0),
    )(par, table)


def forward_kernel(step, first, outs, fold, weighted, marks, own, north, south, weights, mix, *rest):
    obs, out = rest if weighted else (None, rest[0])
    shape = own.shape[1:]
    rightward = right_lanes(shape)
    mixing = mix[step][:, : shape[0]]
    blocks = []
    for p in range(outs):
        way = jnp.broadcast_to(marks[first + p][step : step + 1].astype(F32), shape)
        stay, up = way == 1, way == 0

        def pick(j):
            return jnp.where(stay, own[j], jnp.where(up, north[j], south[j]))

        left = p - 1 if p > 0 else outs
        right = p + 1 if p < outs - 1 else outs
        edges = jnp.where(rightward, pick(right), pick(left))
        window = jnp.concatenate([pick(p), edges], axis=1)
        interp = jnp.dot(window, window_weights(weights[step, first + p]), preferred_element_type=F32).astype(BF16)
        mixed = jnp.dot(mixing, interp, preferred_element_type=F32).astype(BF16)
        if weighted:
            mixed = (obs[p].astype(F32) * mixed.astype(F32)).astype(BF16)
        if fold and p in (0, outs - 1):
            blocks.append(mixed)
        else:
            out[p - 1 if fold else p] = mixed
    if fold:
        out[outs - 2] = jnp.where(rightward, blocks[1], blocks[0])


def forward(step, outs, fold, marks, rows, weights, mix, obs=None):
    levels, cols = rows[0].shape[1:]
    first = (marks.shape[0] - outs) // 2
    made = outs - 1 if fold else outs
    weighted = obs is not None
    args = (marks, *rows, weights, mix) + ((obs,) if weighted else ())
    return pl.pallas_call(
        functools.partial(forward_kernel, step, first, outs, fold, weighted),
        out_shape=jax.ShapeDtypeStruct((made, levels, cols), BF16),
        in_specs=[VMEM] * len(args),
        out_specs=VMEM,
        compiler_params=pltpu.CompilerParams(vmem_limit_bytes=LIMIT),
        cost_estimate=pl.CostEstimate(flops=outs * 6_000_000, bytes_accessed=2_000_000, transcendentals=0),
    )(*args)


def adjoint_kernel(step, first, reads, summed, marks, *rest):
    parts, (weights, mix, to_north, stay, to_south, spreads) = rest[: 3 if summed else 1], rest[3 if summed else 1 :]
    shape = parts[0].shape[1:]
    cols = shape[1]
    rightward = right_lanes(shape)
    mixing = mix[step].astype(F32).T[: shape[0]].astype(BF16)
    for p in range(reads):
        if summed:
            cot = (parts[0][p] + parts[1][p].astype(F32) + parts[2][p].astype(F32)).astype(BF16)
        else:
            cot = parts[0][p]
        back = jnp.dot(mixing, cot, preferred_element_type=F32).astype(BF16)
        spreads[p] = jnp.dot(back, weights[step, first + p], preferred_element_type=F32)
    nothing = jnp.zeros(shape, F32)

    def way(p):
        return jnp.broadcast_to(marks[first + p][step : step + 1].astype(F32), shape)

    for p in range(1, reads - 1):
        main, to = spreads[p, :, :cols], way(p)
        edges = jnp.where(rightward, spreads[p - 1, :, cols:], spreads[p + 1, :, cols:])
        edges_to = jnp.where(rightward, way(p - 1), way(p + 1))
        total = [jnp.where(to == i, main, nothing) + jnp.where(edges_to == i, edges, nothing) for i in range(3)]
        to_north[p - 1] = total[0].astype(BF16)
        stay[p - 1] = total[1]
        to_south[p - 1] = total[2].astype(BF16)


def adjoint(step, marks, parts, weights, mix):
    reads, levels, cols = parts[0].shape
    first = (marks.shape[0] - reads) // 2
    gives = (reads - 2, levels, cols)
    return pl.pallas_call(
        functools.partial(adjoint_kernel, step, first, reads, len(parts) == 3),
        out_shape=[jax.ShapeDtypeStruct(gives, BF16), jax.ShapeDtypeStruct(gives, F32), jax.ShapeDtypeStruct(gives, BF16)],
        in_specs=[VMEM] * (len(parts) + 3),
        out_specs=[VMEM] * 3,
        scratch_shapes=[pltpu.VMEM((reads, levels, 2 * cols), F32)],
        compiler_params=pltpu.CompilerParams(vmem_limit_bytes=LIMIT),
        cost_estimate=pl.CostEstimate(flops=reads * 6_000_000, bytes_accessed=2_000_000, transcendentals=0),
    )(marks, *parts, weights, mix)


def homes():
    rows, blocks = lax.axis_size("lat"), lax.axis_size("lon")

    def home(row, block):
        half, z = divmod(row, rows // 2)
        column, tracer = divmod(block, RUN)
        return place(rows, blocks, z, column, tracer, half)

    return rows, blocks, home


def place(rows, blocks, z, column, y, core):
    upper, y = divmod(y, RUN // 2)
    return (upper * (rows // 2) + z) * blocks + column * RUN + y * 2 + core


def move(value, pairs):
    return lax.ppermute(value, ("lat", "lon"), pairs)


def from_lat(value, by):
    rows, blocks, home = homes()
    return move(value, [(home(r, b), home(r - by, b)) for r in range(rows) for b in range(blocks) if 0 <= r - by < rows])


def from_lon(value, by):
    rows, blocks, home = homes()
    return move(value, [(home(r, b), home(r, (b - by) % blocks)) for r in range(rows) for b in range(blocks)])


def along_y(value):
    rows, blocks, _ = homes()
    groups = [
        [place(rows, blocks, z, column, y, core) for y in range(RUN)]
        for z in range(rows // 2)
        for column in range(blocks // RUN)
        for core in range(2)
    ]
    return lax.all_to_all(value, ("lat", "lon"), 0, 0, axis_index_groups=groups)


def swap_cores(value, first):
    keep, give = jnp.where(first, value[0], value[1]), jnp.where(first, value[1], value[0])
    blocks = lax.axis_size("lon")
    both = lax.all_gather(give, "lon", axis_index_groups=[[i, i + 1] for i in range(0, blocks, 2)])
    return jnp.where(first, keep, both[0]), jnp.where(first, both[1], keep)


def on_device(vector, obs_weight, departures, weight_index, interp_table, column_mix):
    run, levels, _, cols = vector.shape
    first = lax.axis_index("lon") % 2 == 0
    steps = column_mix.shape[0]
    count = 2 * steps
    share = -(-levels // 16) * 8
    mine = (lax.axis_index("lon") & run - 1).reshape(1)
    bundle = along_y(
        bundled(
            mine, share, departures.reshape(-1), weight_index.reshape(-1), vector[:, :, 0], obs_weight[:, 0], column_mix[:, 0]
        )
    )
    halves = swap_cores(bundle.reshape(2, run // 2, *bundle.shape[1:]), first)
    mix = jnp.concatenate([halves[0][:, -share:], halves[1][:, share - levels :]], axis=1)
    bundle = jnp.stack([half[:, :-share] for half in halves], axis=1).reshape(run, -1, cols)
    marked = levels + count
    state, obs = bundle[:, :levels], bundle[:, marked:]
    reach = steps
    west, east = from_lon(bundle[-reach:, :marked], -run), from_lon(bundle[:reach, :marked], run)

    marks = jnp.concatenate([part[:, levels:marked] for part in (west, bundle, east)])
    par = jnp.max(marks.astype(F32), axis=2).astype(jnp.int32)
    weights = choose(par, interp_table, reach, lambda step: 1 + step)
    turned = choose(par, turn(interp_table), reach, lambda step: reach - 1 - step)
    outer = jnp.where(right_lanes((levels, cols)), east[-1, :levels], west[0, :levels])
    state = jnp.concatenate([west[1:, :levels], state, east[:-1, :levels], outer[None]])
    for step in range(reach):
        last = step == reach - 1
        rows = (state, from_lat(state, -1), from_lat(state, 1))
        state = forward(step, run + 2 * (reach - 1 - step), not last, marks, rows, weights, mix, obs if last else None)

    west, east = from_lon(state[-reach:], -run), from_lon(state[:reach], run)
    parts = (jnp.concatenate([west, state, east]),)
    for step in reversed(range(reach)):
        north, stay, south = adjoint(step, marks, parts, turned, mix)
        parts = (stay, from_lat(north, 1), from_lat(south, -1))
    cot = sum(part.astype(F32) for part in parts).astype(BF16)
    cot = cot.reshape(run // 2, 2, levels, cols)
    lower, upper = swap_cores((cot[:, 0], cot[:, 1]), first)
    return along_y(jnp.concatenate([lower, upper]))[:, :, None]


def solution(mesh):
    placed = (
        P(None, None, "lat", "lon"),
        P(None, "lat", "lon"),
        P(None, "lat", "lon"),
        P(None, "lat", "lon"),
        P(),
        P(None, "lat", None, None),
    )
    return jax.shard_map(
        on_device, mesh=mesh, in_specs=placed, out_specs=P(None, None, "lat", "lon"), check_vma=False
    )
```

```python
import functools

import jax
import jax.numpy as jnp
from jax import lax
from jax.experimental import pallas as pl
from jax.experimental.pallas import tpu as pltpu
from jax.sharding import PartitionSpec as P

F32, BF16 = jnp.float32, jnp.bfloat16
VMEM = pl.BlockSpec(memory_space=pltpu.VMEM)
SMEM = pl.BlockSpec(memory_space=pltpu.SMEM)
LIMIT = 24 * 1024 * 1024
RUN = 8


def right_lanes(shape):
    return lax.broadcasted_iota(jnp.int32, shape, 1) < shape[1] // 2


def bundle_kernel(mine, *refs):
    given, out, held, done = refs[:5], refs[5], refs[6:11], refs[11]
    copies = [pltpu.make_async_copy(given[i], held[i], done.at[i]) for i in range(5)]
    for copy in copies:
        copy.start()
    for copy in copies:
        copy.wait()
    departures, weight_index, vector, obs, mix = held
    run, levels, cols = vector.shape
    marks = [jnp.full((1, cols), ref[i]) for ref in (departures, weight_index) for i in range(ref.shape[0])]
    part = mix[mine[0] >> 1].astype(F32)
    share = out.shape[1] - 2 * levels - len(marks)
    part = jnp.where((mine[0] & 1) == 0, part[:share], part[levels - share :])
    part = jnp.concatenate([part, jnp.zeros((share, cols - levels), F32)], axis=1)
    shared = jnp.concatenate([jnp.concatenate(marks).astype(F32), obs[...], part])
    for tracer in range(run):
        out[tracer] = jnp.concatenate([vector[tracer].astype(F32), shared]).astype(BF16)


def bundled(mine, share, departures, weight_index, vector, obs, mix):
    run, levels, cols = vector.shape
    rows = 2 * levels + departures.shape[0] + weight_index.shape[0] + share
    spaces = (pltpu.SMEM, pltpu.SMEM, pltpu.VMEM, pltpu.VMEM, pltpu.VMEM)
    given = (departures, weight_index, vector, obs, mix)
    return pl.pallas_call(
        bundle_kernel,
        out_shape=jax.ShapeDtypeStruct((run, rows, cols), BF16),
        in_specs=[SMEM] + [pl.BlockSpec(memory_space=pltpu.HBM)] * 5,
        out_specs=VMEM,
        scratch_shapes=[space(x.shape, x.dtype) for space, x in zip(spaces, given)] + [pltpu.SemaphoreType.DMA((5,))],
        compiler_params=pltpu.CompilerParams(vmem_limit_bytes=60 * 1024 * 1024),
        cost_estimate=pl.CostEstimate(flops=0, bytes_accessed=1_000_000, transcendentals=0),
    )(mine, *given)


def window_weights(weights):
    cols = weights.shape[1]
    reach = (weights.shape[0] - cols) // 2
    gap = jnp.zeros((cols - 2 * reach, cols), weights.dtype)
    return jnp.concatenate([weights[reach : reach + cols], weights[reach + cols :], gap, weights[:reach]], axis=0)


def turn_kernel(table, out):
    for i in range(table.shape[0]):
        out[i] = window_weights(table[i]).astype(F32).T.astype(BF16)


def turn(table):
    count, _, cols = table.shape
    return pl.pallas_call(
        turn_kernel,
        out_shape=jax.ShapeDtypeStruct((count, cols, 2 * cols), BF16),
        in_specs=[VMEM],
        out_specs=VMEM,
        compiler_params=pltpu.CompilerParams(vmem_limit_bytes=LIMIT),
        cost_estimate=pl.CostEstimate(flops=0, bytes_accessed=6_000_000, transcendentals=0),
    )(table)


def choose_kernel(outside, par, table, out):
    steps, blocks = out.shape[:2]
    for step in range(steps):
        for p in range(outside(step), blocks - outside(step)):
            out[step, p] = table[par[p, par.shape[1] // 2 + step]]


def choose(par, table, steps, outside):
    return pl.pallas_call(
        functools.partial(choose_kernel, outside),
        out_shape=jax.ShapeDtypeStruct((steps, par.shape[0], *table.shape[1:]), BF16),
        in_specs=[SMEM, VMEM],
        out_specs=VMEM,
        compiler_params=pltpu.CompilerParams(vmem_limit_bytes=LIMIT),
        cost_estimate=pl.CostEstimate(flops=0, bytes_accessed=6_000_000, transcendentals=0),
    )(par, table)


def forward_kernel(step, first, outs, fold, marks, own, north, south, weights, mix, out):
    shape = own.shape[1:]
    rightward = right_lanes(shape)
    mixing = mix[step][:, : shape[0]]
    blocks = []
    for p in range(outs):
        way = jnp.broadcast_to(marks[first + p][step : step + 1].astype(F32), shape)
        stay, up = way == 1, way == 0

        def pick(j):
            return jnp.where(stay, own[j], jnp.where(up, north[j], south[j]))

        left = p - 1 if p > 0 else outs
        right = p + 1 if p < outs - 1 else outs
        edges = jnp.where(rightward, pick(right), pick(left))
        window = jnp.concatenate([pick(p), edges], axis=1)
        interp = jnp.dot(window, window_weights(weights[step, first + p]), preferred_element_type=F32).astype(BF16)
        mixed = jnp.dot(mixing, interp, preferred_element_type=F32).astype(BF16)
        if fold and p in (0, outs - 1):
            blocks.append(mixed)
        else:
            out[p - 1 if fold else p] = mixed
    if fold:
        out[outs - 2] = jnp.where(rightward, blocks[1], blocks[0])


def forward(step, outs, fold, marks, rows, weights, mix):
    levels, cols = rows[0].shape[1:]
    first = (marks.shape[0] - outs) // 2
    made = outs - 1 if fold else outs
    args = (marks, *rows, weights, mix)
    return pl.pallas_call(
        functools.partial(forward_kernel, step, first, outs, fold),
        out_shape=jax.ShapeDtypeStruct((made, levels, cols), BF16),
        in_specs=[VMEM] * len(args),
        out_specs=VMEM,
        compiler_params=pltpu.CompilerParams(vmem_limit_bytes=LIMIT),
        cost_estimate=pl.CostEstimate(flops=outs * 6_000_000, bytes_accessed=2_000_000, transcendentals=0),
    )(*args)


def adjoint_kernel(step, first, reads, summed, marks, *rest):
    parts, (weights, mix, to_north, stay, to_south, spreads) = rest[: 3 if summed else 1], rest[3 if summed else 1 :]
    shape = parts[0].shape[1:]
    cols = shape[1]
    rightward = right_lanes(shape)
    mixing = mix[step].astype(F32).T[: shape[0]].astype(BF16)
    for p in range(reads):
        if summed:
            cot = (parts[0][p] + parts[1][p].astype(F32) + parts[2][p].astype(F32)).astype(BF16)
        else:
            cot = parts[0][p]
        back = jnp.dot(mixing, cot, preferred_element_type=F32).astype(BF16)
        spreads[p] = jnp.dot(back, weights[step, first + p], preferred_element_type=F32)
    nothing = jnp.zeros(shape, F32)

    def way(p):
        return jnp.broadcast_to(marks[first + p][step : step + 1].astype(F32), shape)

    for p in range(1, reads - 1):
        main, to = spreads[p, :, :cols], way(p)
        edges = jnp.where(rightward, spreads[p - 1, :, cols:], spreads[p + 1, :, cols:])
        edges_to = jnp.where(rightward, way(p - 1), way(p + 1))
        total = [jnp.where(to == i, main, nothing) + jnp.where(edges_to == i, edges, nothing) for i in range(3)]
        to_north[p - 1] = total[0].astype(BF16)
        stay[p - 1] = total[1]
        to_south[p - 1] = total[2].astype(BF16)


def adjoint(step, marks, parts, weights, mix):
    reads, levels, cols = parts[0].shape
    first = (marks.shape[0] - reads) // 2
    gives = (reads - 2, levels, cols)
    return pl.pallas_call(
        functools.partial(adjoint_kernel, step, first, reads, len(parts) == 3),
        out_shape=[jax.ShapeDtypeStruct(gives, BF16), jax.ShapeDtypeStruct(gives, F32), jax.ShapeDtypeStruct(gives, BF16)],
        in_specs=[VMEM] * (len(parts) + 3),
        out_specs=[VMEM] * 3,
        scratch_shapes=[pltpu.VMEM((reads, levels, 2 * cols), F32)],
        compiler_params=pltpu.CompilerParams(vmem_limit_bytes=LIMIT),
        cost_estimate=pl.CostEstimate(flops=reads * 6_000_000, bytes_accessed=2_000_000, transcendentals=0),
    )(marks, *parts, weights, mix)


def middle_kernel(step, par, line, above, beside, below, table, turned, out, spreads):
    reads = spreads.shape[0]
    shape = line.shape[1:]
    levels, cols = shape
    rightward = right_lanes(shape)
    rows = (above, beside, below)
    marks = [jnp.concatenate([row[reads + 1].astype(F32), row[reads + 2].astype(F32)]) for row in rows]
    mixing = [row[reads][:, :levels] for row in rows]
    unmixing = [row[reads].astype(F32).T[:levels].astype(BF16) for row in rows]
    count = 2 * (step + 1)
    for p in range(reads):
        left = p - 1 if p > 0 else reads
        right = p + 1 if p < reads - 1 else reads
        window = jnp.concatenate([line[p], jnp.where(rightward, line[right], line[left])], axis=1)
        total = jnp.zeros((levels, 2 * cols), F32)
        for i, row in enumerate(rows):
            which = par[i, p]
            interp = jnp.dot(window, window_weights(table[which]), preferred_element_type=F32).astype(BF16)
            mixed = jnp.dot(mixing[i], interp, preferred_element_type=F32).astype(BF16)
            cot = row[p].astype(F32) * mixed.astype(F32)
            way = jnp.broadcast_to(marks[i][count * p + step : count * p + step + 1], shape)
            cot = jnp.where(way == 2 - i, cot, 0.0).astype(BF16)
            back = jnp.dot(unmixing[i], cot, preferred_element_type=F32).astype(BF16)
            total += jnp.dot(back, turned[which], preferred_element_type=F32)
        spreads[p] = total
    for p in range(1, reads - 1):
        edges = jnp.where(rightward, spreads[p - 1, :, cols:], spreads[p + 1, :, cols:])
        out[p - 1] = (spreads[p, :, :cols] + edges).astype(BF16)


def middle(step, par, line, rows, table, turned):
    reads, (levels, cols) = par.shape[1], line.shape[1:]
    return pl.pallas_call(
        functools.partial(middle_kernel, step),
        out_shape=jax.ShapeDtypeStruct((reads - 2, levels, cols), BF16),
        in_specs=[SMEM] + [VMEM] * 6,
        out_specs=VMEM,
        scratch_shapes=[pltpu.VMEM((reads, levels, 2 * cols), F32)],
        compiler_params=pltpu.CompilerParams(vmem_limit_bytes=LIMIT),
        cost_estimate=pl.CostEstimate(flops=reads * 30_000_000, bytes_accessed=4_000_000, transcendentals=0),
    )(par, line, *rows, table, turned)


def homes():
    rows, blocks = lax.axis_size("lat"), lax.axis_size("lon")

    def home(row, block):
        half, z = divmod(row, rows // 2)
        column, tracer = divmod(block, RUN)
        return place(rows, blocks, z, column, tracer, half)

    return rows, blocks, home


def place(rows, blocks, z, column, y, core):
    upper, y = divmod(y, RUN // 2)
    return (upper * (rows // 2) + z) * blocks + column * RUN + y * 2 + core


def move(value, pairs):
    return lax.ppermute(value, ("lat", "lon"), pairs)


def from_lat(value, by):
    rows, blocks, home = homes()
    return move(value, [(home(r, b), home(r - by, b)) for r in range(rows) for b in range(blocks) if 0 <= r - by < rows])


def from_lon(value, by):
    rows, blocks, home = homes()
    return move(value, [(home(r, b), home(r, (b - by) % blocks)) for r in range(rows) for b in range(blocks)])


def along_y(value):
    rows, blocks, _ = homes()
    groups = [
        [place(rows, blocks, z, column, y, core) for y in range(RUN)]
        for z in range(rows // 2)
        for column in range(blocks // RUN)
        for core in range(2)
    ]
    return lax.all_to_all(value, ("lat", "lon"), 0, 0, axis_index_groups=groups)


def swap_cores(value, first):
    keep, give = jnp.where(first, value[0], value[1]), jnp.where(first, value[1], value[0])
    blocks = lax.axis_size("lon")
    both = lax.all_gather(give, "lon", axis_index_groups=[[i, i + 1] for i in range(0, blocks, 2)])
    return jnp.where(first, keep, both[0]), jnp.where(first, both[1], keep)


def on_device(vector, obs_weight, departures, weight_index, interp_table, column_mix):
    run, levels, _, cols = vector.shape
    first = lax.axis_index("lon") % 2 == 0
    steps = column_mix.shape[0]
    count = 2 * steps
    share = -(-levels // 16) * 8
    mine = (lax.axis_index("lon") & run - 1).reshape(1)
    bundle = along_y(
        bundled(
            mine, share, departures.reshape(-1), weight_index.reshape(-1), vector[:, :, 0], obs_weight[:, 0], column_mix[:, 0]
        )
    )
    halves = swap_cores(bundle.reshape(2, run // 2, *bundle.shape[1:]), first)
    mix = jnp.concatenate([halves[0][:, -share:], halves[1][:, share - levels :]], axis=1)
    bundle = jnp.stack([half[:, :-share] for half in halves], axis=1).reshape(run, -1, cols)
    marked = levels + count
    reach = steps
    west, east = from_lon(bundle[-reach:], -run), from_lon(bundle[:reach], run)
    line = jnp.concatenate([west, bundle, east])
    marks = line[:, levels:marked]
    par = jnp.max(marks.astype(F32), axis=2).astype(jnp.int32)
    last = steps - 1
    weights = choose(par, interp_table, last, lambda step: 2 + step)
    table = turn(interp_table)
    turned = choose(par, table, last, lambda step: reach - 1 - step)

    span = line.shape[0]
    room = -(-span * count // levels) * levels - span * count
    flat = jnp.concatenate([marks.reshape(-1, cols), jnp.zeros((room, cols), BF16)]).reshape(-1, levels, cols)
    beside = jnp.concatenate([line[:, marked:], mix[last][None], flat])
    cuts = (0, 4, 10, beside.shape[0])

    outer = jnp.where(right_lanes((levels, cols)), line[-2, :levels], line[1, :levels])
    state = jnp.concatenate([line[2:-2, :levels], outer[None]])
    above, below = [], []
    for step in range(last):
        sent = jnp.concatenate([state, beside[cuts[step] : cuts[step + 1]]])
        north, south = from_lat(sent, -1), from_lat(sent, 1)
        above.append(north[state.shape[0] :])
        below.append(south[state.shape[0] :])
        outs = run + 2 * (last - 1 - step)
        state = forward(step, outs, step < last - 1, marks, (state, north, south), weights, mix)

    west, east = from_lon(state[-reach - 1 :], -run), from_lon(state[: reach + 1], run)
    outer = jnp.where(right_lanes((levels, cols)), east[-1], west[0])
    line = jnp.concatenate([west[1:], state, east[:-1], outer[None]])
    rows = (jnp.concatenate(above), beside, jnp.concatenate(below))

    def chosen(row):
        numbers = row[span + 1 :].reshape(-1, cols)[: span * count].reshape(span, count, cols)[:, -1]
        return jnp.max(numbers.astype(F32), axis=1).astype(jnp.int32)

    par = jnp.stack([chosen(row) for row in rows])
    parts = (middle(last, par, line, rows, interp_table, table),)
    for step in reversed(range(last)):
        north, stay, south = adjoint(step, marks, parts, turned, mix)
        parts = (stay, from_lat(north, 1), from_lat(south, -1))
    cot = sum(part.astype(F32) for part in parts).astype(BF16)
    cot = cot.reshape(run // 2, 2, levels, cols)
    lower, upper = swap_cores((cot[:, 0], cot[:, 1]), first)
    return along_y(jnp.concatenate([lower, upper]))[:, :, None]


def solution(mesh):
    placed = (
        P(None, None, "lat", "lon"),
        P(None, "lat", "lon"),
        P(None, "lat", "lon"),
        P(None, "lat", "lon"),
        P(),
        P(None, "lat", None, None),
    )
    return jax.shard_map(
        on_device, mesh=mesh, in_specs=placed, out_specs=P(None, None, "lat", "lon"), check_vma=False
    )
```

```python
import functools

import jax
import jax.numpy as jnp
from jax import lax
from jax.experimental import pallas as pl
from jax.experimental.pallas import tpu as pltpu
from jax.sharding import PartitionSpec as P

F32, BF16 = jnp.float32, jnp.bfloat16
VMEM = pl.BlockSpec(memory_space=pltpu.VMEM)
SMEM = pl.BlockSpec(memory_space=pltpu.SMEM)
LIMIT = 24 * 1024 * 1024
RUN = 8


def right_lanes(shape):
    return lax.broadcasted_iota(jnp.int32, shape, 1) < shape[1] // 2


def bundle_kernel(mine, *refs):
    given, out, held, done = refs[:5], refs[5], refs[6:11], refs[11]
    copies = [pltpu.make_async_copy(given[i], held[i], done.at[i]) for i in range(5)]
    for copy in copies:
        copy.start()
    for copy in copies:
        copy.wait()
    departures, weight_index, vector, obs, mix = held
    run, levels, cols = vector.shape
    marks = [jnp.full((1, cols), ref[i]) for ref in (departures, weight_index) for i in range(ref.shape[0])]
    part = mix[mine[0] >> 1].astype(F32)
    share = out.shape[1] - 2 * levels - len(marks)
    part = jnp.where((mine[0] & 1) == 0, part[:share], part[levels - share :])
    part = jnp.concatenate([part, jnp.zeros((share, cols - levels), F32)], axis=1)
    shared = jnp.concatenate([jnp.concatenate(marks).astype(F32), obs[...], part])
    for tracer in range(run):
        out[tracer] = jnp.concatenate([vector[tracer].astype(F32), shared]).astype(BF16)


def bundled(mine, share, departures, weight_index, vector, obs, mix):
    run, levels, cols = vector.shape
    rows = 2 * levels + departures.shape[0] + weight_index.shape[0] + share
    spaces = (pltpu.SMEM, pltpu.SMEM, pltpu.VMEM, pltpu.VMEM, pltpu.VMEM)
    given = (departures, weight_index, vector, obs, mix)
    return pl.pallas_call(
        bundle_kernel,
        out_shape=jax.ShapeDtypeStruct((run, rows, cols), BF16),
        in_specs=[SMEM] + [pl.BlockSpec(memory_space=pltpu.HBM)] * 5,
        out_specs=VMEM,
        scratch_shapes=[space(x.shape, x.dtype) for space, x in zip(spaces, given)] + [pltpu.SemaphoreType.DMA((5,))],
        compiler_params=pltpu.CompilerParams(vmem_limit_bytes=60 * 1024 * 1024),
        cost_estimate=pl.CostEstimate(flops=0, bytes_accessed=1_000_000, transcendentals=0),
    )(mine, *given)


def window_weights(weights):
    cols = weights.shape[1]
    reach = (weights.shape[0] - cols) // 2
    gap = jnp.zeros((cols - 2 * reach, cols), weights.dtype)
    return jnp.concatenate([weights[reach : reach + cols], weights[reach + cols :], gap, weights[:reach]], axis=0)


def turn_kernel(table, out):
    for i in range(table.shape[0]):
        out[i] = window_weights(table[i]).astype(F32).T.astype(BF16)


def turn(table):
    count, _, cols = table.shape
    return pl.pallas_call(
        turn_kernel,
        out_shape=jax.ShapeDtypeStruct((count, cols, 2 * cols), BF16),
        in_specs=[VMEM],
        out_specs=VMEM,
        compiler_params=pltpu.CompilerParams(vmem_limit_bytes=LIMIT),
        cost_estimate=pl.CostEstimate(flops=0, bytes_accessed=6_000_000, transcendentals=0),
    )(table)


def choose_kernel(outside, par, table, out):
    steps, blocks = out.shape[:2]
    for step in range(steps):
        for p in range(outside(step), blocks - outside(step)):
            out[step, p] = table[par[p, par.shape[1] // 2 + step]]


def choose(par, table, steps, outside):
    return pl.pallas_call(
        functools.partial(choose_kernel, outside),
        out_shape=jax.ShapeDtypeStruct((steps, par.shape[0], *table.shape[1:]), BF16),
        in_specs=[SMEM, VMEM],
        out_specs=VMEM,
        compiler_params=pltpu.CompilerParams(vmem_limit_bytes=LIMIT),
        cost_estimate=pl.CostEstimate(flops=0, bytes_accessed=6_000_000, transcendentals=0),
    )(par, table)


def forward_kernel(step, first, outs, fold, marks, own, north, south, weights, mix, out):
    shape = own.shape[1:]
    rightward = right_lanes(shape)
    mixing = mix[step][:, : shape[0]]
    blocks = []
    for p in range(outs):
        way = jnp.broadcast_to(marks[first + p][step : step + 1].astype(F32), shape)
        stay, up = way == 1, way == 0

        def pick(j):
            return jnp.where(stay, own[j], jnp.where(up, north[j], south[j]))

        left = p - 1 if p > 0 else outs
        right = p + 1 if p < outs - 1 else outs
        edges = jnp.where(rightward, pick(right), pick(left))
        window = jnp.concatenate([pick(p), edges], axis=1)
        interp = jnp.dot(window, window_weights(weights[step, first + p]), preferred_element_type=F32).astype(BF16)
        mixed = jnp.dot(mixing, interp, preferred_element_type=F32).astype(BF16)
        if fold and p in (0, outs - 1):
            blocks.append(mixed)
        else:
            out[p - 1 if fold else p] = mixed
    if fold:
        out[outs - 2] = jnp.where(rightward, blocks[1], blocks[0])


def forward(step, outs, fold, marks, rows, weights, mix):
    levels, cols = rows[0].shape[1:]
    first = (marks.shape[0] - outs) // 2
    made = outs - 1 if fold else outs
    args = (marks, *rows, weights, mix)
    return pl.pallas_call(
        functools.partial(forward_kernel, step, first, outs, fold),
        out_shape=jax.ShapeDtypeStruct((made, levels, cols), BF16),
        in_specs=[VMEM] * len(args),
        out_specs=VMEM,
        compiler_params=pltpu.CompilerParams(vmem_limit_bytes=LIMIT),
        cost_estimate=pl.CostEstimate(flops=outs * 6_000_000, bytes_accessed=2_000_000, transcendentals=0),
    )(*args)


def adjoint_kernel(step, first, reads, summed, marks, *rest):
    parts, (weights, mix, to_north, stay, to_south, spreads) = rest[: 3 if summed else 1], rest[3 if summed else 1 :]
    shape = parts[0].shape[1:]
    cols = shape[1]
    rightward = right_lanes(shape)
    mixing = mix[step].astype(F32).T[: shape[0]].astype(BF16)
    for p in range(reads):
        if summed:
            cot = (parts[0][p] + parts[1][p].astype(F32) + parts[2][p].astype(F32)).astype(BF16)
        else:
            cot = parts[0][p]
        back = jnp.dot(mixing, cot, preferred_element_type=F32).astype(BF16)
        spreads[p] = jnp.dot(back, weights[step, first + p], preferred_element_type=F32)
    nothing = jnp.zeros(shape, F32)

    def way(p):
        return jnp.broadcast_to(marks[first + p][step : step + 1].astype(F32), shape)

    for p in range(1, reads - 1):
        main, to = spreads[p, :, :cols], way(p)
        edges = jnp.where(rightward, spreads[p - 1, :, cols:], spreads[p + 1, :, cols:])
        edges_to = jnp.where(rightward, way(p - 1), way(p + 1))
        total = [jnp.where(to == i, main, nothing) + jnp.where(edges_to == i, edges, nothing) for i in range(3)]
        to_north[p - 1] = total[0].astype(BF16)
        stay[p - 1] = total[1]
        to_south[p - 1] = total[2].astype(BF16)


def adjoint(step, marks, parts, weights, mix):
    reads, levels, cols = parts[0].shape
    first = (marks.shape[0] - reads) // 2
    gives = (reads - 2, levels, cols)
    return pl.pallas_call(
        functools.partial(adjoint_kernel, step, first, reads, len(parts) == 3),
        out_shape=[jax.ShapeDtypeStruct(gives, BF16), jax.ShapeDtypeStruct(gives, F32), jax.ShapeDtypeStruct(gives, BF16)],
        in_specs=[VMEM] * (len(parts) + 3),
        out_specs=[VMEM] * 3,
        scratch_shapes=[pltpu.VMEM((reads, levels, 2 * cols), F32)],
        compiler_params=pltpu.CompilerParams(vmem_limit_bytes=LIMIT),
        cost_estimate=pl.CostEstimate(flops=reads * 6_000_000, bytes_accessed=2_000_000, transcendentals=0),
    )(marks, *parts, weights, mix)


def middle_kernel(step, par, line, above, beside, below, marks, table, turned, out, cots, spreads):
    reads = spreads.shape[0]
    shape = line.shape[1:]
    levels, cols = shape
    rightward = right_lanes(shape)
    for i, row in enumerate((above, beside, below)):
        mixing = row[reads][:, :levels]
        unmixing = row[reads].astype(F32).T[:levels].astype(BF16)
        for p in range(reads):
            left = p - 1 if p > 0 else reads
            right = p + 1 if p < reads - 1 else reads
            window = jnp.concatenate([line[p], jnp.where(rightward, line[right], line[left])], axis=1)
            weights = window_weights(table[par[i, p]])
            interp = jnp.dot(window, weights, preferred_element_type=F32).astype(BF16)
            mixed = jnp.dot(mixing, interp, preferred_element_type=F32).astype(BF16)
            way = jnp.broadcast_to(marks[i, p][step : step + 1].astype(F32), shape)
            cot = row[p].astype(F32) * mixed.astype(F32)
            cots[p] = jnp.where(way == 2 - i, cot, 0.0).astype(BF16)
        for p in range(reads):
            back = jnp.dot(unmixing, cots[p], preferred_element_type=F32).astype(BF16)
            spread = jnp.dot(back, turned[par[i, p]], preferred_element_type=F32)
            spreads[p] = spread if i == 0 else spreads[p] + spread
    for p in range(1, reads - 1):
        edges = jnp.where(rightward, spreads[p - 1, :, cols:], spreads[p + 1, :, cols:])
        out[p - 1] = (spreads[p, :, :cols] + edges).astype(BF16)


def middle(step, par, line, rows, marks, table, turned):
    reads, (levels, cols) = par.shape[1], line.shape[1:]
    return pl.pallas_call(
        functools.partial(middle_kernel, step),
        out_shape=jax.ShapeDtypeStruct((reads - 2, levels, cols), BF16),
        in_specs=[SMEM] + [VMEM] * 7,
        out_specs=VMEM,
        scratch_shapes=[pltpu.VMEM((reads, levels, cols), BF16), pltpu.VMEM((reads, levels, 2 * cols), F32)],
        compiler_params=pltpu.CompilerParams(vmem_limit_bytes=LIMIT),
        cost_estimate=pl.CostEstimate(flops=reads * 30_000_000, bytes_accessed=4_000_000, transcendentals=0),
    )(par, line, *rows, marks, table, turned)


def homes():
    rows, blocks = lax.axis_size("lat"), lax.axis_size("lon")

    def home(row, block):
        half, z = divmod(row, rows // 2)
        column, tracer = divmod(block, RUN)
        return place(rows, blocks, z, column, tracer, half)

    return rows, blocks, home


def place(rows, blocks, z, column, y, core):
    upper, y = divmod(y, RUN // 2)
    return (upper * (rows // 2) + z) * blocks + column * RUN + y * 2 + core


def move(value, pairs):
    return lax.ppermute(value, ("lat", "lon"), pairs)


def from_lat(value, by):
    rows, blocks, home = homes()
    return move(value, [(home(r, b), home(r - by, b)) for r in range(rows) for b in range(blocks) if 0 <= r - by < rows])


def from_lon(value, by):
    rows, blocks, home = homes()
    return move(value, [(home(r, b), home(r, (b - by) % blocks)) for r in range(rows) for b in range(blocks)])


def along_y(value):
    rows, blocks, _ = homes()
    groups = [
        [place(rows, blocks, z, column, y, core) for y in range(RUN)]
        for z in range(rows // 2)
        for column in range(blocks // RUN)
        for core in range(2)
    ]
    return lax.all_to_all(value, ("lat", "lon"), 0, 0, axis_index_groups=groups)


def swap_cores(value, first):
    keep, give = jnp.where(first, value[0], value[1]), jnp.where(first, value[1], value[0])
    blocks = lax.axis_size("lon")
    both = lax.all_gather(give, "lon", axis_index_groups=[[i, i + 1] for i in range(0, blocks, 2)])
    return jnp.where(first, keep, both[0]), jnp.where(first, both[1], keep)


def on_device(vector, obs_weight, departures, weight_index, interp_table, column_mix):
    run, levels, _, cols = vector.shape
    first = lax.axis_index("lon") % 2 == 0
    steps = column_mix.shape[0]
    count = 2 * steps
    share = -(-levels // 16) * 8
    mine = (lax.axis_index("lon") & run - 1).reshape(1)
    bundle = along_y(
        bundled(
            mine, share, departures.reshape(-1), weight_index.reshape(-1), vector[:, :, 0], obs_weight[:, 0], column_mix[:, 0]
        )
    )
    halves = swap_cores(bundle.reshape(2, run // 2, *bundle.shape[1:]), first)
    mix = jnp.concatenate([halves[0][:, -share:], halves[1][:, share - levels :]], axis=1)
    bundle = jnp.stack([half[:, :-share] for half in halves], axis=1).reshape(run, -1, cols)
    marked = levels + count
    reach = steps
    west, east = from_lon(bundle[-reach:], -run), from_lon(bundle[:reach], run)
    line = jnp.concatenate([west, bundle, east])
    marks = line[:, levels:marked]
    par = jnp.max(marks.astype(F32), axis=2).astype(jnp.int32)
    last = steps - 1
    weights = choose(par, interp_table, last, lambda step: 2 + step)
    table = turn(interp_table)
    turned = choose(par, table, last, lambda step: reach - 1 - step)

    span = line.shape[0]
    room = -(-span * count // levels) * levels - span * count
    flat = jnp.concatenate([marks.reshape(-1, cols), jnp.zeros((room, cols), BF16)]).reshape(-1, levels, cols)
    beside = jnp.concatenate([line[:, marked:], mix[last][None], flat])
    cuts = (0, 4, 10, beside.shape[0])

    outer = jnp.where(right_lanes((levels, cols)), line[-2, :levels], line[1, :levels])
    state = jnp.concatenate([line[2:-2, :levels], outer[None]])
    above, below = [], []
    for step in range(last):
        sent = jnp.concatenate([state, beside[cuts[step] : cuts[step + 1]]])
        north, south = from_lat(sent, -1), from_lat(sent, 1)
        above.append(north[state.shape[0] :])
        below.append(south[state.shape[0] :])
        outs = run + 2 * (last - 1 - step)
        state = forward(step, outs, step < last - 1, marks, (state, north, south), weights, mix)

    west, east = from_lon(state[-reach - 1 :], -run), from_lon(state[: reach + 1], run)
    outer = jnp.where(right_lanes((levels, cols)), east[-1], west[0])
    line = jnp.concatenate([west[1:], state, east[:-1], outer[None]])
    rows = (jnp.concatenate(above), beside, jnp.concatenate(below))

    marks_of = jnp.stack([row[span + 1 :].reshape(-1, cols)[: span * count].reshape(span, count, cols) for row in rows])
    par = jnp.max(marks_of[:, :, -1].astype(F32), axis=2).astype(jnp.int32)
    parts = (middle(last, par, line, rows, marks_of, interp_table, table),)
    for step in reversed(range(last)):
        north, stay, south = adjoint(step, marks, parts, turned, mix)
        parts = (stay, from_lat(north, 1), from_lat(south, -1))
    cot = sum(part.astype(F32) for part in parts).astype(BF16)
    cot = cot.reshape(run // 2, 2, levels, cols)
    lower, upper = swap_cores((cot[:, 0], cot[:, 1]), first)
    return along_y(jnp.concatenate([lower, upper]))[:, :, None]


def solution(mesh):
    placed = (
        P(None, None, "lat", "lon"),
        P(None, "lat", "lon"),
        P(None, "lat", "lon"),
        P(None, "lat", "lon"),
        P(),
        P(None, "lat", None, None),
    )
    return jax.shard_map(
        on_device, mesh=mesh, in_specs=placed, out_specs=P(None, None, "lat", "lon"), check_vma=False
    )
```

```python
import functools

import jax
import jax.numpy as jnp
from jax import lax
from jax.experimental import pallas as pl
from jax.experimental.pallas import tpu as pltpu
from jax.sharding import PartitionSpec as P

F32, BF16 = jnp.float32, jnp.bfloat16
VMEM = pl.BlockSpec(memory_space=pltpu.VMEM)
SMEM = pl.BlockSpec(memory_space=pltpu.SMEM)
LIMIT = 24 * 1024 * 1024
RUN = 8


def right_lanes(shape):
    return lax.broadcasted_iota(jnp.int32, shape, 1) < shape[1] // 2


def bundle_kernel(mine, *refs):
    given, out, held, done = refs[:5], refs[5], refs[6:11], refs[11]
    copies = [pltpu.make_async_copy(given[i], held[i], done.at[i]) for i in range(5)]
    for copy in copies:
        copy.start()
    for copy in copies:
        copy.wait()
    departures, weight_index, vector, obs, mix = held
    run, levels, cols = vector.shape
    marks = [jnp.full((1, cols), ref[i]) for ref in (departures, weight_index) for i in range(ref.shape[0])]
    part = mix[mine[0] >> 1].astype(F32)
    share = out.shape[1] - 2 * levels - len(marks)
    part = jnp.where((mine[0] & 1) == 0, part[:share], part[levels - share :])
    part = jnp.concatenate([part, jnp.zeros((share, cols - levels), F32)], axis=1)
    shared = jnp.concatenate([jnp.concatenate(marks).astype(F32), obs[...], part])
    for tracer in range(run):
        out[tracer] = jnp.concatenate([vector[tracer].astype(F32), shared]).astype(BF16)


def bundled(mine, share, departures, weight_index, vector, obs, mix):
    run, levels, cols = vector.shape
    rows = 2 * levels + departures.shape[0] + weight_index.shape[0] + share
    spaces = (pltpu.SMEM, pltpu.SMEM, pltpu.VMEM, pltpu.VMEM, pltpu.VMEM)
    given = (departures, weight_index, vector, obs, mix)
    return pl.pallas_call(
        bundle_kernel,
        out_shape=jax.ShapeDtypeStruct((run, rows, cols), BF16),
        in_specs=[SMEM] + [pl.BlockSpec(memory_space=pltpu.HBM)] * 5,
        out_specs=VMEM,
        scratch_shapes=[space(x.shape, x.dtype) for space, x in zip(spaces, given)] + [pltpu.SemaphoreType.DMA((5,))],
        compiler_params=pltpu.CompilerParams(vmem_limit_bytes=60 * 1024 * 1024),
        cost_estimate=pl.CostEstimate(flops=0, bytes_accessed=1_000_000, transcendentals=0),
    )(mine, *given)


def window_weights(weights):
    cols = weights.shape[1]
    reach = (weights.shape[0] - cols) // 2
    gap = jnp.zeros((cols - 2 * reach, cols), weights.dtype)
    return jnp.concatenate([weights[reach : reach + cols], weights[reach + cols :], gap, weights[:reach]], axis=0)


def turn_kernel(table, out):
    for i in range(table.shape[0]):
        out[i] = window_weights(table[i]).astype(F32).T.astype(BF16)


def turn(table):
    count, _, cols = table.shape
    return pl.pallas_call(
        turn_kernel,
        out_shape=jax.ShapeDtypeStruct((count, cols, 2 * cols), BF16),
        in_specs=[VMEM],
        out_specs=VMEM,
        compiler_params=pltpu.CompilerParams(vmem_limit_bytes=LIMIT),
        cost_estimate=pl.CostEstimate(flops=0, bytes_accessed=6_000_000, transcendentals=0),
    )(table)


def choose_kernel(outside, par, table, out):
    steps, blocks = out.shape[:2]
    for step in range(steps):
        for p in range(outside(step), blocks - outside(step)):
            out[step, p] = table[par[p, par.shape[1] // 2 + step]]


def choose(par, table, steps, outside):
    return pl.pallas_call(
        functools.partial(choose_kernel, outside),
        out_shape=jax.ShapeDtypeStruct((steps, par.shape[0], *table.shape[1:]), BF16),
        in_specs=[SMEM, VMEM],
        out_specs=VMEM,
        compiler_params=pltpu.CompilerParams(vmem_limit_bytes=LIMIT),
        cost_estimate=pl.CostEstimate(flops=0, bytes_accessed=6_000_000, transcendentals=0),
    )(par, table)


def forward_kernel(step, first, outs, fold, marks, own, north, south, weights, mix, out):
    shape = own.shape[1:]
    rightward = right_lanes(shape)
    mixing = mix[step][:, : shape[0]]
    blocks = []
    for p in range(outs):
        way = jnp.broadcast_to(marks[first + p][step : step + 1].astype(F32), shape)
        stay, up = way == 1, way == 0

        def pick(j):
            return jnp.where(stay, own[j], jnp.where(up, north[j], south[j]))

        left = p - 1 if p > 0 else outs
        right = p + 1 if p < outs - 1 else outs
        edges = jnp.where(rightward, pick(right), pick(left))
        window = jnp.concatenate([pick(p), edges], axis=1)
        interp = jnp.dot(window, window_weights(weights[step, first + p]), preferred_element_type=F32).astype(BF16)
        mixed = jnp.dot(mixing, interp, preferred_element_type=F32).astype(BF16)
        if fold and p in (0, outs - 1):
            blocks.append(mixed)
        else:
            out[p - 1 if fold else p] = mixed
    if fold:
        out[outs - 2] = jnp.where(rightward, blocks[1], blocks[0])


def forward(step, outs, fold, marks, rows, weights, mix):
    levels, cols = rows[0].shape[1:]
    first = (marks.shape[0] - outs) // 2
    made = outs - 1 if fold else outs
    args = (marks, *rows, weights, mix)
    return pl.pallas_call(
        functools.partial(forward_kernel, step, first, outs, fold),
        out_shape=jax.ShapeDtypeStruct((made, levels, cols), BF16),
        in_specs=[VMEM] * len(args),
        out_specs=VMEM,
        compiler_params=pltpu.CompilerParams(vmem_limit_bytes=LIMIT),
        cost_estimate=pl.CostEstimate(flops=outs * 6_000_000, bytes_accessed=2_000_000, transcendentals=0),
    )(*args)


def adjoint_kernel(step, first, reads, summed, marks, *rest):
    parts, (weights, mix, to_north, stay, to_south, spreads) = rest[: 3 if summed else 1], rest[3 if summed else 1 :]
    shape = parts[0].shape[1:]
    cols = shape[1]
    rightward = right_lanes(shape)
    mixing = mix[step].astype(F32).T[: shape[0]].astype(BF16)
    for p in range(reads):
        if summed:
            cot = (parts[0][p] + parts[1][p].astype(F32) + parts[2][p].astype(F32)).astype(BF16)
        else:
            cot = parts[0][p]
        back = jnp.dot(mixing, cot, preferred_element_type=F32).astype(BF16)
        spreads[p] = jnp.dot(back, weights[step, first + p], preferred_element_type=F32)
    nothing = jnp.zeros(shape, F32)

    def way(p):
        return jnp.broadcast_to(marks[first + p][step : step + 1].astype(F32), shape)

    for p in range(1, reads - 1):
        main, to = spreads[p, :, :cols], way(p)
        edges = jnp.where(rightward, spreads[p - 1, :, cols:], spreads[p + 1, :, cols:])
        edges_to = jnp.where(rightward, way(p - 1), way(p + 1))
        total = [jnp.where(to == i, main, nothing) + jnp.where(edges_to == i, edges, nothing) for i in range(3)]
        to_north[p - 1] = total[0].astype(BF16)
        stay[p - 1] = total[1]
        to_south[p - 1] = total[2].astype(BF16)


def adjoint(step, marks, parts, weights, mix):
    reads, levels, cols = parts[0].shape
    first = (marks.shape[0] - reads) // 2
    gives = (reads - 2, levels, cols)
    return pl.pallas_call(
        functools.partial(adjoint_kernel, step, first, reads, len(parts) == 3),
        out_shape=[jax.ShapeDtypeStruct(gives, BF16), jax.ShapeDtypeStruct(gives, F32), jax.ShapeDtypeStruct(gives, BF16)],
        in_specs=[VMEM] * (len(parts) + 3),
        out_specs=[VMEM] * 3,
        scratch_shapes=[pltpu.VMEM((reads, levels, 2 * cols), F32)],
        compiler_params=pltpu.CompilerParams(vmem_limit_bytes=LIMIT),
        cost_estimate=pl.CostEstimate(flops=reads * 6_000_000, bytes_accessed=2_000_000, transcendentals=0),
    )(marks, *parts, weights, mix)


def middle_kernel(step, par, line, above, beside, below, marks, table, turned, out, cots, spreads):
    reads = spreads.shape[0]
    shape = line.shape[1:]
    levels, cols = shape
    rightward = right_lanes(shape)
    for i, row in enumerate((above, beside, below)):
        mixing = row[reads][:, :levels]
        unmixing = row[reads].astype(F32).T[:levels].astype(BF16)
        for p in range(reads):
            left = p - 1 if p > 0 else reads
            right = p + 1 if p < reads - 1 else reads
            window = jnp.concatenate([line[p], jnp.where(rightward, line[right], line[left])], axis=1)
            weights = window_weights(table[par[i, p]])
            interp = jnp.dot(window, weights, preferred_element_type=F32).astype(BF16)
            mixed = jnp.dot(mixing, interp, preferred_element_type=F32).astype(BF16)
            way = jnp.broadcast_to(marks[i, p][step : step + 1].astype(F32), shape)
            cot = row[p].astype(F32) * mixed.astype(F32)
            cots[p] = jnp.where(way == 2 - i, cot, 0.0).astype(BF16)
        for p in range(reads):
            back = jnp.dot(unmixing, cots[p], preferred_element_type=F32).astype(BF16)
            spread = jnp.dot(back, turned[par[i, p]], preferred_element_type=F32)
            spreads[p] = spread if i == 0 else spreads[p] + spread
    for p in range(1, reads - 1):
        edges = jnp.where(rightward, spreads[p - 1, :, cols:], spreads[p + 1, :, cols:])
        out[p - 1] = (spreads[p, :, :cols] + edges).astype(BF16)


def middle(step, par, line, rows, marks, table, turned):
    reads, (levels, cols) = par.shape[1], line.shape[1:]
    return pl.pallas_call(
        functools.partial(middle_kernel, step),
        out_shape=jax.ShapeDtypeStruct((reads - 2, levels, cols), BF16),
        in_specs=[SMEM] + [VMEM] * 7,
        out_specs=VMEM,
        scratch_shapes=[pltpu.VMEM((reads, levels, cols), BF16), pltpu.VMEM((reads, levels, 2 * cols), F32)],
        compiler_params=pltpu.CompilerParams(vmem_limit_bytes=LIMIT),
        cost_estimate=pl.CostEstimate(flops=reads * 30_000_000, bytes_accessed=4_000_000, transcendentals=0),
    )(par, line, *rows, marks, table, turned)


def homes():
    rows, blocks = lax.axis_size("lat"), lax.axis_size("lon")

    def home(row, block):
        half, z = divmod(row, rows // 2)
        column, tracer = divmod(block, RUN)
        return place(rows, blocks, z, column, tracer, half)

    return rows, blocks, home


def place(rows, blocks, z, column, y, core):
    upper, y = divmod(y, RUN // 2)
    return (upper * (rows // 2) + z) * blocks + column * RUN + y * 2 + core


def move(value, pairs):
    return lax.ppermute(value, ("lat", "lon"), pairs)


def from_lat(value, by):
    rows, blocks, home = homes()
    return move(value, [(home(r, b), home(r - by, b)) for r in range(rows) for b in range(blocks) if 0 <= r - by < rows])


def from_lon(value, by):
    rows, blocks, home = homes()
    return move(value, [(home(r, b), home(r, (b - by) % blocks)) for r in range(rows) for b in range(blocks)])


def along_y(value):
    rows, blocks, _ = homes()
    groups = [
        [place(rows, blocks, z, column, y, core) for y in range(RUN)]
        for z in range(rows // 2)
        for column in range(blocks // RUN)
        for core in range(2)
    ]
    return lax.all_to_all(value, ("lat", "lon"), 0, 0, axis_index_groups=groups)


def swap_cores(value, first):
    keep, give = jnp.where(first, value[0], value[1]), jnp.where(first, value[1], value[0])
    blocks = lax.axis_size("lon")
    both = lax.all_gather(give, "lon", axis_index_groups=[[i, i + 1] for i in range(0, blocks, 2)])
    return jnp.where(first, keep, both[0]), jnp.where(first, both[1], keep)


def on_device(vector, obs_weight, departures, weight_index, interp_table, column_mix):
    run, levels, _, cols = vector.shape
    first = lax.axis_index("lon") % 2 == 0
    steps = column_mix.shape[0]
    count = 2 * steps
    share = -(-levels // 16) * 8
    mine = (lax.axis_index("lon") & run - 1).reshape(1)
    bundle = along_y(
        bundled(
            mine, share, departures.reshape(-1), weight_index.reshape(-1), vector[:, :, 0], obs_weight[:, 0], column_mix[:, 0]
        )
    )
    halves = swap_cores(bundle.reshape(2, run // 2, *bundle.shape[1:]), first)
    mix = jnp.concatenate([halves[0][:, -share:], halves[1][:, share - levels :]], axis=1)
    bundle = jnp.stack([half[:, :-share] for half in halves], axis=1).reshape(run, -1, cols)
    marked = levels + count
    reach = steps
    west, east = from_lon(bundle[-reach:], -run), from_lon(bundle[:reach], run)
    line = jnp.concatenate([west, bundle, east])
    marks = line[:, levels:marked]
    par = jnp.max(marks.astype(F32), axis=2).astype(jnp.int32)
    last = steps - 1
    weights = choose(par, interp_table, last, lambda step: 2 + step)

    span = line.shape[0]
    room = -(-span * count // levels) * levels - span * count
    flat = jnp.concatenate([marks.reshape(-1, cols), jnp.zeros((room, cols), BF16)]).reshape(-1, levels, cols)
    beside = jnp.concatenate([line[:, marked:], mix[last][None], flat])
    cuts = (0, 4, 10, beside.shape[0])

    outer = jnp.where(right_lanes((levels, cols)), line[-2, :levels], line[1, :levels])
    state = jnp.concatenate([line[2:-2, :levels], outer[None]])
    above, below = [], []
    for step in range(last):
        sent = jnp.concatenate([state, beside[cuts[step] : cuts[step + 1]]])
        north, south = from_lat(sent, -1), from_lat(sent, 1)
        above.append(north[state.shape[0] :])
        below.append(south[state.shape[0] :])
        outs = run + 2 * (last - 1 - step)
        state = forward(step, outs, step < last - 1, marks, (state, north, south), weights, mix)

    state, par, raw = lax.optimization_barrier((state, par, interp_table))
    west, east = from_lon(state[-reach - 1 :], -run), from_lon(state[: reach + 1], run)
    table = turn(raw)
    turned = choose(par, table, last, lambda step: reach - 1 - step)
    outer = jnp.where(right_lanes((levels, cols)), east[-1], west[0])
    line = jnp.concatenate([west[1:], state, east[:-1], outer[None]])
    rows = (jnp.concatenate(above), beside, jnp.concatenate(below))

    marks_of = jnp.stack([row[span + 1 :].reshape(-1, cols)[: span * count].reshape(span, count, cols) for row in rows])
    par = jnp.max(marks_of[:, :, -1].astype(F32), axis=2).astype(jnp.int32)
    parts = (middle(last, par, line, rows, marks_of, interp_table, table),)
    for step in reversed(range(last)):
        north, stay, south = adjoint(step, marks, parts, turned, mix)
        parts = (stay, from_lat(north, 1), from_lat(south, -1))
    cot = sum(part.astype(F32) for part in parts).astype(BF16)
    cot = cot.reshape(run // 2, 2, levels, cols)
    lower, upper = swap_cores((cot[:, 0], cot[:, 1]), first)
    return along_y(jnp.concatenate([lower, upper]))[:, :, None]


def solution(mesh):
    placed = (
        P(None, None, "lat", "lon"),
        P(None, "lat", "lon"),
        P(None, "lat", "lon"),
        P(None, "lat", "lon"),
        P(),
        P(None, "lat", None, None),
    )
    return jax.shard_map(
        on_device, mesh=mesh, in_specs=placed, out_specs=P(None, None, "lat", "lon"), check_vma=False
    )
```
